512 devices in a mesh: rep: 8 (over z_lo, core), fsdp: 64 (over z_hi, x, y).
Axes of the slice: x: 4, y: 4, z: 16 (z_hi: 4, z_lo: 4; z = z_hi * 4 + z_lo), core: 2. Of those that a mesh axis runs over, the one named last changes fastest.
Arguments:
- gu_pseudo: bfloat16 [8, 64, 2, 4, 28672], P('rep', 'fsdp'), may hold values from -6 to 6
- gu_master: float32 [2, 4, 28672], P(None, None, 'fsdp'), may hold values from -6 to 6
- gu_moment: float32 [2, 4, 28672], P(None, None, 'fsdp'), may hold values from -6 to 6
- down_pseudo: bfloat16 [8, 64, 64, 8192], P('rep', 'fsdp'), may hold values from -6 to 6
- down_master: float32 [64, 8192], P(None, 'fsdp'), may hold values from -6 to 6
- down_moment: float32 [64, 8192], P(None, 'fsdp'), may hold values from -6 to 6
Outputs:
- gu_params: bfloat16 [2, 4, 28672], replicated
- down_params: bfloat16 [64, 8192], replicated
- gu_master_new: float32 [2, 4, 28672], P(None, None, 'fsdp')
- down_master_new: float32 [64, 8192], P(None, 'fsdp')
- gu_moment_new: float32 [2, 4, 28672], P(None, None, 'fsdp')
- down_moment_new: float32 [64, 8192], P(None, 'fsdp')
- gu_scale: float32 [2, 4, 448], P(None, None, 'fsdp')
- down_scale: float32 [64, 128], P(None, 'fsdp')
The draws below stay inside these ranges and needn't reach their ends.
All inputs are finite; a program needn't handle non-finite values. Where the reference program divides by a largest or mean magnitude, that divisor is 1e-20 or more.
Results may differ from the reference program's by a relative error of at most 0.015.
Values may be sent and summed in bfloat16 or wider, within the bound.
A program may use at most 128 MiB of HBM per device.

```python
import jax
import jax.numpy as jnp
from jax import lax

D = 8192
FF = 28672
GR = 4
DR = 64
BLOCK = 64
N_REP = 8
N_FSDP = 64


def strengthened(drawn, own_key, source, target, shards_of, factor):
    def block_of(axis_at):
        return (jnp.arange(drawn.shape[axis_at]) // (drawn.shape[axis_at] // shards_of)).reshape((-1,) + (1,) * (drawn.ndim - 1 - axis_at))

    first = jax.random.permutation(own_key, shards_of)[block_of(target)]
    other_side = (block_of(target) + shards_of // 2) % shards_of
    return jnp.where((block_of(source) == first) | (block_of(source) == other_side), factor * drawn, drawn)


def block_levels(key, dims, cuts, least, high):
    factor_of = 1.0
    for dim, shards_of in cuts:
        heights = jax.random.uniform(jax.random.fold_in(jax.random.fold_in(key, 6), dim), (shards_of,), jnp.float32, least / len(cuts), high / len(cuts))
        factor_of = factor_of * jnp.repeat(jnp.exp(heights), dims[dim] // shards_of).reshape((-1,) + (1,) * (len(dims) - 1 - dim))
    return factor_of


def centred(key, extent, scale, bound, pieces=(), held_as=jnp.bfloat16):
    array = jax.random.normal(key, extent, jnp.float32) * scale
    if len(pieces) > 0:
        array = block_levels(key, extent, pieces, -0.22, 0.18) * array
    return jnp.clip(array, min=-bound, max=bound).astype(held_as)


def heavy_noise(stream_key, extent, width, limit, pieces, heavy, held_as=jnp.bfloat16):
    values = width * jax.random.normal(stream_key, extent, jnp.float32)
    if pieces:
        values = values * block_levels(stream_key, extent, pieces, -0.22, 0.18)
    return jnp.clip(strengthened(values, jax.random.fold_in(stream_key, 3), *heavy), -limit, limit).astype(held_as)


def setup_inputs(seed: int = 0) -> dict:
    streams_of = jax.random.split(jax.random.key(seed), 7)
    gu_pseudo = heavy_noise(streams_of[0], (N_REP, N_FSDP, 2, GR, FF), 0.35, 6.0, ((0, 8), (1, 64)), (1, 4, 64, 4.0))
    gu_master = centred(streams_of[1], (2, GR, FF), 1.0, 6.0, ((2, 64),), jnp.float32)
    gu_moment = centred(streams_of[2], (2, GR, FF), 1.0, 6.0, ((2, 64),), jnp.float32)
    down_pseudo = heavy_noise(streams_of[3], (N_REP, N_FSDP, DR, D), 0.35, 6.0, ((0, 8), (1, 64)), (1, 3, 64, 4.0))
    down_master = centred(streams_of[4], (DR, D), 1.0, 6.0, ((1, 64),), jnp.float32)
    down_moment = centred(streams_of[5], (DR, D), 1.0, 6.0, ((1, 64),), jnp.float32)
    return {"gu_pseudo": gu_pseudo, "gu_master": gu_master, "gu_moment": gu_moment, "down_pseudo": down_pseudo, "down_master": down_master, "down_moment": down_moment}


def outer_group(pseudo, master, moment):
    partial_value = lax.map(lambda piece: jnp.sum(piece.astype(jnp.float32), axis=0), pseudo)
    shape = partial_value.shape
    blocks = partial_value.reshape(shape[:-1] + (shape[-1] // BLOCK, BLOCK))
    scale = jnp.max(jnp.max(jnp.abs(blocks), axis=-1), axis=0) + 1e-6
    coded = (blocks / scale[..., None]).astype(jnp.bfloat16)
    coded = lax.optimization_barrier(coded).astype(jnp.float32)
    total = jnp.sum(coded, axis=0)
    delta = (scale[..., None] * total).reshape(shape[1:]) / N_REP
    moment_new = 0.9 * moment + delta
    master_new = master - 0.7 * (delta + 0.9 * moment_new)
    return master_new.astype(jnp.bfloat16), master_new, moment_new, scale


def reference(gu_pseudo, gu_master, gu_moment, down_pseudo, down_master, down_moment):
    gu_params, gu_master_new, gu_moment_new, gu_scale = outer_group(gu_pseudo, gu_master, gu_moment)
    down_params, down_master_new, down_moment_new, down_scale = outer_group(down_pseudo, down_master, down_moment)
    return (gu_params, down_params, gu_master_new, down_master_new, gu_moment_new, down_moment_new, gu_scale, down_scale)
```

```python
import functools

import jax
import jax.numpy as jnp
from jax import lax
from jax.experimental import pallas as pl
from jax.experimental.pallas import tpu as pltpu
from jax.sharding import PartitionSpec as P

NX = 4
NY = 4
ZH = 4
ZL = 4
LANES = 128
HALF = 64
GUCOLS = 448
TILES = 6
BF = jnp.bfloat16
F32 = jnp.float32

S1, S2, S3, SD, SG0, SG1, SG2, SC = 0, 2, 4, 5, 6, 7, 9, 11
NSEM = 13


def kernel(
    gu_ref, gm_ref, gmo_ref, dn_ref, dm_ref, dmo_ref,
    gu_out, dn_out, gm_out, dm_out, gmo_out, dmo_out, gs_out, ds_out,
    S, R1, PS, R2, Q, R3, D, G, M, MO, send, recv,
):
    rep = lax.axis_index("rep")
    fsdp = lax.axis_index("fsdp")
    zl, core = rep // 2, rep % 2
    zh, x, y = fsdp // (NX * NY), (fsdp // NY) % NX, fsdp % NY
    z = zh * ZL + zl
    along = ((x, y), (y, x))

    def fs(zh_, x_, y_):
        return (zh_ * NX + x_) * NY + y_

    def first_peer(h, d):
        return fs(zh, d, y) if h == 0 else fs(zh, x, d)

    def second_peer(h, d):
        return fs(zh, x, d) if h == 0 else fs(zh, d, y)

    def remote(src, dst, sem, rep_, fsdp_):
        return pltpu.make_async_remote_copy(
            src_ref=src, dst_ref=dst, send_sem=send.at[sem], recv_sem=recv.at[sem],
            device_id={"rep": rep_, "fsdp": fsdp_}, device_id_type=pl.DeviceIdType.MESH,
        )

    def wait_bytes(ref, sem):
        pltpu.make_async_copy(ref, ref, sem).wait()

    barrier = pltpu.get_barrier_semaphore()

    def greet(rep_, fsdp_):
        pl.semaphore_signal(
            barrier, inc=1, device_id={"rep": rep_, "fsdp": fsdp_},
            device_id_type=pl.DeviceIdType.MESH,
        )

    for d in range(1, 4):
        greet(rep, fs(zh, (x + d) % 4, y))
        greet(rep, fs(zh, x, (y + d) % 4))

    def greet_line(k, carry):
        other = (z * 2 + core + k) % 32
        oz = other // 2
        greet((oz % ZL) * 2 + other % 2, fs(oz // ZL, x, y))
        return carry

    lax.fori_loop(1, 32, greet_line, 0)

    lane = lax.broadcasted_iota(jnp.int32, (8, 512), 1)
    for zh_ in range(ZH):
        h, z2 = zh_ // 2, zh_ % 2
        for x_ in range(NX):
            for y_ in range(NY):
                d1, d2 = (x_, y_) if h == 0 else (y_, x_)
                col = ((zh_ * NX + x_) * NY + y_) * LANES
                S[h, d1, d2, z2, 0:64, :] = dn_ref[0, 0, :, col : col + LANES]
            for yp in range(NY // 2):
                col = ((zh_ * NX + x_) * NY + 2 * yp) * GUCOLS
                both = jnp.concatenate(
                    [gu_ref[0, 0, g, :, col : col + 2 * GUCOLS].astype(F32) for g in range(2)], axis=0
                )
                odd = pltpu.roll(both[:, 384:896], 512 - HALF, 1)
                for o, part in enumerate((both[:, 0:512], odd)):
                    part = jnp.where(lane < GUCOLS, part, 0.0)
                    y_ = 2 * yp + o
                    d1, d2 = (x_, y_) if h == 0 else (y_, x_)
                    for t in range(2):
                        two = jnp.concatenate(
                            [part[:, 256 * t : 256 * t + 128], part[:, 256 * t + 128 : 256 * t + 256]], axis=0
                        )
                        S[h, d1, d2, z2, 64 + 16 * t : 80 + 16 * t, :] = two.astype(BF)
    for g_ref, d_ref, out in ((gm_ref, dm_ref, M), (gmo_ref, dmo_ref, MO)):
        for j in range(4):
            out[j] = d_ref[16 * j : 16 * j + 16, :]
        for g in range(2):
            for t in range(4):
                row = 8 * (t % 2) + 4 * g
                if t < 3:
                    out[4 + t // 2, row : row + 4, :] = g_ref[g, :, 128 * t : 128 * t + 128]
                else:
                    out[5, row : row + 4, :] = jnp.concatenate(
                        [g_ref[g, :, 384:448], jnp.zeros((4, HALF), F32)], axis=1
                    )

    pl.semaphore_wait(barrier, 37)

    for d in range(1, 4):
        for h in range(2):
            dest = (along[h][0] + d) % 4
            remote(S.at[h, dest], R1.at[h, d - 1], S1 + h, rep, first_peer(h, dest)).start()
    for h in range(2):
        mine, other = along[h]
        wait_bytes(R1.at[h], recv.at[S1 + h])
        for d in (1, 2, 3, 0):
            dest = (other + d) % 4
            acc = S[h, mine, dest].astype(F32)
            for i in range(3):
                acc = acc + R1[h, i, dest].astype(F32)
            PS[h, dest] = acc.astype(BF)
            if d:
                remote(PS.at[h, dest], R2.at[h, d - 1], S2 + h, rep, second_peer(h, dest)).start()
    for h in range(2):
        _, other = along[h]
        wait_bytes(R2.at[h], recv.at[S2 + h])
        acc = PS[h, other].astype(F32)
        for i in range(3):
            acc = acc + R2[h, i].astype(F32)
        Q[2 * h : 2 * h + 2] = acc.astype(BF).reshape(2, TILES, 16, LANES)

    for dz in range(4):
        to = (zh + dz) % 4
        for j in range(TILES):
            copy = remote(Q.at[to, j], R3.at[zh * 8 + rep], S3, j, fs(to, x, y))
            if dz:
                copy.start()
            else:
                pl.when(rep != j)(copy.start)

    @pl.when(rep < TILES)
    def _():
        R3[zh * 8 + rep] = Q[zh, rep]
        wait_bytes(R3.at[pl.ds(0, 31)], recv.at[S3])
        largest = jnp.zeros((16, LANES), F32)
        total = jnp.zeros((16, LANES), F32)
        for r in range(8):
            part = R3[r].astype(F32)
            for k in range(1, 4):
                part = part + R3[8 * k + r].astype(F32)
            largest = jnp.maximum(largest, jnp.abs(part))
            total = total + part
        low = lax.broadcasted_iota(jnp.int32, (16, LANES), 1) < HALF
        low_max = jnp.max(jnp.where(low, largest, 0.0), axis=1, keepdims=True)
        high_max = jnp.max(jnp.where(low, 0.0, largest), axis=1, keepdims=True)
        delta = total / 8
        D[rep, 0] = delta
        D[rep, 1] = jnp.where(low, low_max, high_max) + 1e-6
        moment = 0.9 * MO[rep] + delta
        master = M[rep] - 0.7 * (delta + 0.9 * moment)
        hh = zh // 2
        d1 = jnp.where(hh == 0, x, y)
        d2 = jnp.where(hh == 0, y, x)
        mine = G.at[core, hh, d1, d2, zh % 2, zl]
        mine[...] = master.astype(BF)

        def spread(k, carry):
            oz = (z + k) % 16
            remote(mine, mine, SG0, (oz % ZL) * 2 + core, fs(oz // ZL, x, y)).start()
            return carry

        lax.fori_loop(1, 16, spread, 0)
        for k in range(1, 8):
            remote(D.at[rep], D.at[rep], SD, (rep + k) % 8, fsdp).start()
        wait_bytes(R3.at[pl.ds(0, 11)], recv.at[SG0])

    @pl.when(rep >= TILES)
    def _():
        wait_bytes(R3.at[pl.ds(0, 12)], recv.at[SG0])

    for h in range(2):
        mine, other = along[h]
        for d in range(1, 4):
            dest = (other + d) % 4
            block = G.at[core, h, mine, other]
            remote(block, block, SG1 + h, rep, second_peer(h, dest)).start()

    @pl.when(rep < TILES)
    def _():
        wait_bytes(D.at[pl.ds(0, 5)], recv.at[SD])

    @pl.when(rep >= TILES)
    def _():
        wait_bytes(D, recv.at[SD])

    low = lax.broadcasted_iota(jnp.int32, (16, LANES), 1)
    moments, masters, scales = [], [], []
    for j in range(TILES):
        moment = 0.9 * MO[j] + D[j, 0]
        moments.append(moment)
        masters.append(M[j] - 0.7 * (D[j, 0] + 0.9 * moment))
        scales.append(D[j, 1])
    for tiles, d_out, g_out in ((moments, dmo_out, gmo_out), (masters, dm_out, gm_out)):
        for j in range(4):
            d_out[16 * j : 16 * j + 16, :] = tiles[j]
        for g in range(2):
            for t in range(4):
                row = 8 * (t % 2) + 4 * g
                width = 128 if t < 3 else 64
                g_out[g, :, 128 * t : 128 * t + width] = tiles[4 + t // 2][row : row + 4, :width]
    for j in range(4):
        pair = jnp.where(low == 0, scales[j], pltpu.roll(scales[j], HALF, 1))
        ds_out[16 * j : 16 * j + 16, :] = pair[:, 0:2]
    lane8 = lax.broadcasted_iota(jnp.int32, (8, LANES), 1)
    acc = jnp.zeros((8, LANES), F32)
    for t in range(4):
        tile = scales[4 + t // 2][8 * (t % 2) : 8 * (t % 2) + 8]
        acc = jnp.where(lane8 == 2 * t, tile, acc)
        acc = jnp.where(lane8 == 2 * t + 1, pltpu.roll(tile, HALF, 1), acc)
    for g in range(2):
        gs_out[g, :, :] = acc[4 * g : 4 * g + 4, 0:7]

    sibling = zl * 2 + (1 - core)
    for h in range(2):
        mine, other = along[h]
        wait_bytes(G.at[core, h, mine, pl.ds(0, 3)], recv.at[SG1 + h])
        block = G.at[core, h, mine]
        for d in range(1, 4):
            dest = (mine + d) % 4
            remote(block, block, SG2 + h, rep, first_peer(h, dest)).start()
        remote(block, block, SC + h, sibling, fsdp).start()
    for h in range(2):
        mine, other = along[h]
        wait_bytes(G.at[core, h, pl.ds(0, 3)], recv.at[SG2 + h])
        for d in range(1, 4):
            block = G.at[core, h, (mine + d) % 4]
            remote(block, block, SC + h, sibling, fsdp).start()
    for h in range(2):
        wait_bytes(G.at[1 - core, h], recv.at[SC + h])
        for z2 in range(2):
            zh_ = 2 * h + z2
            for x_ in range(NX):
                gu_tiles = []
                for y_ in range(NY):
                    d1, d2 = (x_, y_) if h == 0 else (y_, x_)
                    col = ((zh_ * NX + x_) * NY + y_) * LANES
                    for j in range(4):
                        dn_out[16 * j : 16 * j + 16, col : col + LANES] = G[j % 2, h, d1, d2, z2, j // 2]
                    wide = []
                    for c in range(2):
                        tile = G[c, h, d1, d2, z2, 2].astype(F32)
                        wide += [tile[0:8], tile[8:16]]
                    gu_tiles.append(wide)
                for yp in range(NY // 2):
                    even, odd = gu_tiles[2 * yp], gu_tiles[2 * yp + 1]
                    odd = pltpu.roll(jnp.concatenate(odd, axis=1), HALF, 1)
                    joined = jnp.where(lane8 < HALF, even[3], odd[:, 0:128])
                    full = jnp.concatenate(even[:3] + [joined, odd[:, 128:512]], axis=1)
                    col = ((zh_ * NX + x_) * NY + 2 * yp) * GUCOLS
                    for g in range(2):
                        gu_out[g, :, col : col + 2 * GUCOLS] = full[4 * g : 4 * g + 4].astype(BF)

    for h in range(2):
        mine, other = along[h]
        wait_bytes(S.at[h, pl.ds(0, 3)], send.at[S1 + h])
        wait_bytes(PS.at[h, pl.ds(0, 3)], send.at[S2 + h])
        wait_bytes(G.at[core, h, mine, pl.ds(0, 3)], send.at[SG1 + h])
        wait_bytes(G.at[core, h, pl.ds(0, 3)], send.at[SG2 + h])
        wait_bytes(G.at[core, h], send.at[SC + h])

    @pl.when(rep < TILES)
    def _():
        wait_bytes(R3.at[pl.ds(0, 23)], send.at[S3])
        wait_bytes(R3.at[pl.ds(0, 15)], send.at[SG0])
        wait_bytes(R3.at[pl.ds(0, 28)], send.at[SD])

    @pl.when(rep >= TILES)
    def _():
        wait_bytes(R3.at[pl.ds(0, 24)], send.at[S3])


def per_device(gu_pseudo, gu_master, gu_moment, down_pseudo, down_master, down_moment):
    full_gu = gu_pseudo.shape[2:]
    full_dn = down_pseudo.shape[2:]
    vmem = pl.BlockSpec(memory_space=pltpu.VMEM)
    return pl.pallas_call(
        kernel,
        out_shape=(
            jax.ShapeDtypeStruct(full_gu, BF),
            jax.ShapeDtypeStruct(full_dn, BF),
            jax.ShapeDtypeStruct(gu_master.shape, F32),
            jax.ShapeDtypeStruct(down_master.shape, F32),
            jax.ShapeDtypeStruct(gu_master.shape, F32),
            jax.ShapeDtypeStruct(down_master.shape, F32),
            jax.ShapeDtypeStruct(gu_master.shape[:2] + (7,), F32),
            jax.ShapeDtypeStruct((down_master.shape[0], 2), F32),
        ),
        in_specs=[vmem] * 6,
        out_specs=[vmem] * 8,
        scratch_shapes=[
            pltpu.VMEM((2, 4, 4, 2, 96, LANES), BF),
            pltpu.VMEM((2, 3, 4, 2, 96, LANES), BF),
            pltpu.VMEM((2, 4, 2, 96, LANES), BF),
            pltpu.VMEM((2, 3, 2, 96, LANES), BF),
            pltpu.VMEM((4, TILES, 16, LANES), BF),
            pltpu.VMEM((32, 16, LANES), BF),
            pltpu.VMEM((TILES, 2, 16, LANES), F32),
            pltpu.VMEM((2, 2, 4, 4, 2, 3, 16, LANES), BF),
            pltpu.VMEM((TILES, 16, LANES), F32),
            pltpu.VMEM((TILES, 16, LANES), F32),
            pltpu.SemaphoreType.DMA((NSEM,)),
            pltpu.SemaphoreType.DMA((NSEM,)),
        ],
        compiler_params=pltpu.CompilerParams(
            collective_id=0, has_side_effects=True, vmem_limit_bytes=32 * 1024 * 1024
        ),
    )(gu_pseudo, gu_master, gu_moment, down_pseudo, down_master, down_moment)


def solution(mesh):
    in_specs = (
        P("rep", "fsdp", None, None, None),
        P(None, None, "fsdp"),
        P(None, None, "fsdp"),
        P("rep", "fsdp", None, None),
        P(None, "fsdp"),
        P(None, "fsdp"),
    )
    out_specs = (
        P(),
        P(),
        P(None, None, "fsdp"),
        P(None, "fsdp"),
        P(None, None, "fsdp"),
        P(None, "fsdp"),
        P(None, None, "fsdp"),
        P(None, "fsdp"),
    )
    return jax.shard_map(
        per_device, mesh=mesh, in_specs=in_specs, out_specs=out_specs, check_vma=False
    )
```

```python
import jax
import jax.numpy as jnp
from jax import lax
from jax.experimental import pallas as pl
from jax.experimental.pallas import tpu as pltpu
from jax.sharding import PartitionSpec as P

NX = 4
NY = 4
ZH = 4
ZL = 4
LANES = 128
HALF = 64
GUCOLS = 448
OWN = 3
BF = jnp.bfloat16
F32 = jnp.float32
MIB = 1024 * 1024

P1A, P1B, P2, Z3, Z0, SD, SDS, A1, A2A, A2B, A2R, SC = 0, 4, 6, 8, 9, 10, 11, 12, 14, 18, 22, 26
NSEM = 28


def kernel(
    gu_ref, gm_ref, gmo_ref, dn_ref, dm_ref, dmo_ref,
    gu_out, dn_out, gm_out, dm_out, gmo_out, dmo_out, gs_out, ds_out,
    gu_in, dn_in, gm_in, gmo_in, dm_in, dmo_in,
    S, RA, R1, PS, R2, Q, R3, D, G, M, MO, send, recv, local,
):
    rep = lax.axis_index("rep")
    fsdp = lax.axis_index("fsdp")
    zl, core = rep // 2, rep % 2
    zh, x, y = fsdp // (NX * NY), (fsdp // NY) % NX, fsdp % NY
    z = zh * ZL + zl
    along = ((x, y), (y, x))
    sibling = zl * 2 + (1 - core)

    def fs(zh_, x_, y_):
        return (zh_ * NX + x_) * NY + y_

    def first_peer(h, d):
        return fs(zh, d, y) if h == 0 else fs(zh, x, d)

    def second_peer(h, d):
        return fs(zh, x, d) if h == 0 else fs(zh, d, y)

    def remote(src, dst, out, sem, rep_, fsdp_):
        return pltpu.make_async_remote_copy(
            src_ref=src, dst_ref=dst, send_sem=send.at[out], recv_sem=recv.at[sem],
            device_id={"rep": rep_, "fsdp": fsdp_}, device_id_type=pl.DeviceIdType.MESH,
        )

    def wait_bytes(ref, sem):
        pltpu.make_async_copy(ref, ref, sem).wait()

    loads = [
        pltpu.make_async_copy(src, dst, local.at[i])
        for i, (src, dst) in enumerate(
            (
                (dn_ref, dn_in), (gu_ref, gu_in), (dm_ref, dm_in), (dmo_ref, dmo_in),
                (gm_ref, gm_in), (gmo_ref, gmo_in),
            )
        )
    ]
    for load in loads:
        load.start()
    barrier = pltpu.get_barrier_semaphore()

    def greet(rep_, fsdp_):
        pl.semaphore_signal(
            barrier, inc=1, device_id={"rep": rep_, "fsdp": fsdp_},
            device_id_type=pl.DeviceIdType.MESH,
        )

    def greet_line(k, carry):
        oz = (z + k) % 16
        greet((oz % ZL) * 2 + core, fs(oz // ZL, x, y))
        return carry

    lax.fori_loop(1, 16, greet_line, 0)
    greet(sibling, fsdp)
    for r in (rep, sibling):
        for d in range(1, 4):
            greet(r, fs(zh, (x + d) % 4, y))
            greet(r, fs(zh, x, (y + d) % 4))

    lane = lax.broadcasted_iota(jnp.int32, (8, 512), 1)
    lane8 = lax.broadcasted_iota(jnp.int32, (8, LANES), 1)
    loads[0].wait()
    for zh_ in range(ZH):
        h, z2 = zh_ // 2, zh_ % 2
        for x_ in range(NX):
            for y_ in range(NY):
                d1, d2 = (x_, y_) if h == 0 else (y_, x_)
                col = ((zh_ * NX + x_) * NY + y_) * LANES
                for c in range(2):
                    S[h, d1, d2, c, z2, 0:32, :] = dn_in[0, 0, 32 * c : 32 * c + 32, col : col + LANES]
    loads[1].wait()
    for zh_ in range(ZH):
        h, z2 = zh_ // 2, zh_ % 2
        for x_ in range(NX):
            for yp in range(NY // 2):
                col = ((zh_ * NX + x_) * NY + 2 * yp) * GUCOLS
                both = jnp.concatenate(
                    [gu_in[0, 0, g, :, col : col + 2 * GUCOLS].astype(F32) for g in range(2)], axis=0
                )
                odd = pltpu.roll(both[:, 384:896], 512 - HALF, 1)
                for o, part in enumerate((both[:, 0:512], odd)):
                    part = jnp.where(lane < GUCOLS, part, 0.0)
                    y_ = 2 * yp + o
                    d1, d2 = (x_, y_) if h == 0 else (y_, x_)
                    for c in range(2):
                        two = jnp.concatenate(
                            [part[:, 256 * c : 256 * c + 128], part[:, 256 * c + 128 : 256 * c + 256]], axis=0
                        )
                        S[h, d1, d2, c, z2, 32:48, :] = two.astype(BF)
    for load in loads[2:]:
        load.wait()
    for g_ref, d_ref, out in ((gm_in, dm_in, M), (gmo_in, dmo_in, MO)):
        for c in range(2):
            for k in range(2):
                row = 32 * c + 16 * k
                out[c, k] = d_ref[row : row + 16, :]
        for g in range(2):
            for t in range(4):
                row = 8 * (t % 2) + 4 * g
                if t < 3:
                    out[t // 2, 2, row : row + 4, :] = g_ref[g, :, 128 * t : 128 * t + 128]
                else:
                    out[1, 2, row : row + 4, :] = jnp.concatenate(
                        [g_ref[g, :, 384:448], jnp.zeros((4, HALF), F32)], axis=1
                    )

    pl.semaphore_wait(barrier, 28)

    def ways(h):
        mine = along[h][0]
        return (
            (0, (mine + 1) % 4, pl.ds(0, 2), pl.ds(2, 2)),
            (1, (mine + 3) % 4, pl.ds(2, 2), pl.ds(0, 2)),
        )

    for h in range(2):
        far = (along[h][0] + 2) % 4
        for w, near, on, _ in ways(h):
            remote(S.at[h, far, on], RA.at[h, w], P1B + h, P1A + 2 * h + w, rep, first_peer(h, near)).start()
    for h in range(2):
        for w, near, _, rest in ways(h):
            remote(S.at[h, near, rest], R1.at[h, w, rest], P1B + h, P1B + h, rep, first_peer(h, near)).start()
    for h in range(2):
        for w, near, on, _ in ways(h):
            wait_bytes(RA.at[h, w], recv.at[P1A + 2 * h + w])
            S[h, near, on] = (S[h, near, on].astype(F32) + RA[h, w].astype(F32)).astype(BF)
            remote(S.at[h, near, on], R1.at[h, w, on], P1B + h, P1B + h, rep, first_peer(h, near)).start()

    for h in range(2):
        mine, other = along[h]
        wait_bytes(R1.at[h], recv.at[P1B + h])
        for d in (2, 1, 3, 0):
            dest = (other + d) % 4
            acc = S[h, mine, dest].astype(F32) + R1[h, 0, dest].astype(F32) + R1[h, 1, dest].astype(F32)
            PS[h, dest] = acc.astype(BF)
            if d:
                to = second_peer(h, dest)
                slot = R2.at[h, 2 * (d - 1) + core]
                remote(PS.at[h, dest, core], slot, P2 + h, P2 + h, rep, to).start()
                remote(PS.at[h, dest, 1 - core], slot, P2 + h, P2 + h, sibling, to).start()
            else:
                remote(PS.at[h, dest, 1 - core], R2.at[h, 6 + core], P2 + h, P2 + h, sibling, fsdp).start()
                R2[h, 6 + core] = PS[h, dest, core]
    for h in range(2):
        wait_bytes(R2.at[h, pl.ds(0, 7)], recv.at[P2 + h])
        for c in range(2):
            acc = R2[h, c].astype(F32)
            for i in range(1, 4):
                acc = acc + R2[h, 2 * i + c].astype(F32)
            acc = acc.astype(BF).reshape(2, OWN, 16, LANES)
            for z2 in range(2):
                for k in range(OWN):
                    Q[2 * h + z2, k, c] = acc[z2, k]
        for z2 in range(2):
            for k in range(OWN):
                to = 2 * h + z2
                copy = remote(Q.at[to, k], R3.at[pl.ds(2 * z, 2)], Z3, Z3, 2 * k + core, fs(to, x, y))
                pl.when(jnp.logical_or(zh != to, zl != k))(copy.start)

    hh = zh // 2
    d1 = jnp.where(hh == 0, x, y)
    d2 = jnp.where(hh == 0, y, x)

    @pl.when(zl < OWN)
    def _():
        R3[pl.ds(2 * z, 2)] = Q[zh, zl]
        wait_bytes(R3.at[pl.ds(0, 30)], recv.at[Z3])
        largest = jnp.zeros((16, LANES), F32)
        total = jnp.zeros((16, LANES), F32)
        for r in range(8):
            part = R3[r].astype(F32)
            for k in range(1, 4):
                part = part + R3[8 * k + r].astype(F32)
            largest = jnp.maximum(largest, jnp.abs(part))
            total = total + part
        delta = total / 8
        moment = 0.9 * MO[core, zl] + delta
        master = M[core, zl] - 0.7 * (delta + 0.9 * moment)
        mine = G.at[core, hh, d1, d2, zh % 2, zl]
        mine[...] = master.astype(BF)

        def spread(k, carry):
            oz = (z + k) % 16
            remote(mine, mine, Z0, Z0, (oz % ZL) * 2 + core, fs(oz // ZL, x, y)).start()
            return carry

        lax.fori_loop(1, 16, spread, 0)
        low = lax.broadcasted_iota(jnp.int32, (16, LANES), 1) < HALF
        low_max = jnp.max(jnp.where(low, largest, 0.0), axis=1, keepdims=True)
        high_max = jnp.max(jnp.where(low, 0.0, largest), axis=1, keepdims=True)
        D[core, zl, 0] = delta
        D[core, zl, 1] = jnp.where(low, low_max, high_max) + 1e-6
        for k in range(1, 4):
            block = D.at[core, zl]
            remote(block, block, SD, SD, ((zl + k) % ZL) * 2 + core, fsdp).start()
        wait_bytes(R3.at[pl.ds(0, 11)], recv.at[Z0])

    @pl.when(zl >= OWN)
    def _():
        wait_bytes(R3.at[pl.ds(0, 12)], recv.at[Z0])

    for h in range(2):
        mine, other = along[h]
        for d in (2, 1, 3):
            dest = (other + d) % 4
            block = G.at[core, h, mine, other]
            remote(block, block, A1 + h, A1 + h, rep, second_peer(h, dest)).start()
    for h in range(2):
        mine, other = along[h]
        wait_bytes(G.at[core, h, mine, pl.ds(0, 3)], recv.at[A1 + h])
        for w, near, on, _ in ways(h):
            block = G.at[core, h, mine, on]
            remote(block, block, A2A + h, A2A + 2 * h + w, rep, first_peer(h, near)).start()
        for w, near, _, rest in ways(h):
            block = G.at[core, h, mine, rest]
            remote(block, block, A2A + h, A2B + 2 * h + w, rep, first_peer(h, near)).start()
        block = G.at[core, h, mine]
        remote(block, block, SC + h, SC + h, sibling, fsdp).start()

    @pl.when(zl < OWN)
    def _():
        wait_bytes(D.at[core, pl.ds(0, 2)], recv.at[SD])

    @pl.when(zl >= OWN)
    def _():
        wait_bytes(D.at[core], recv.at[SD])

    remote(D.at[core], D.at[core], SDS, SDS, sibling, fsdp).start()

    for h in range(2):
        back = ways(h)[1][1], ways(h)[0][1]
        for w, near, on, _ in ways(h):
            block = G.at[core, h, back[w], on]
            wait_bytes(block, recv.at[A2A + 2 * h + w])
            remote(block, block, A2A + h, A2R + 2 * h + w, rep, first_peer(h, near)).start()
            remote(block, block, SC + h, SC + h, sibling, fsdp).start()

    wait_bytes(D.at[1 - core], recv.at[SDS])
    state = ([], [], [])
    for c in range(2):
        for k in range(OWN):
            moment = 0.9 * MO[c, k] + D[c, k, 0]
            state[0].append(moment)
            state[1].append(M[c, k] - 0.7 * (D[c, k, 0] + 0.9 * moment))
            state[2].append(D[c, k, 1])
    moments, masters, scales = ([s[0:3], s[3:6]] for s in state)
    for tiles, d_out, g_out in ((moments, dmo_out, gmo_out), (masters, dm_out, gm_out)):
        for c in range(2):
            for k in range(2):
                row = 32 * c + 16 * k
                d_out[row : row + 16, :] = tiles[c][k]
        for g in range(2):
            for t in range(4):
                row = 8 * (t % 2) + 4 * g
                width = 128 if t < 3 else 64
                g_out[g, :, 128 * t : 128 * t + width] = tiles[t // 2][2][row : row + 4, :width]
    rows = jnp.concatenate([scales[c][k] for c in range(2) for k in range(2)], axis=0)
    lane64 = lax.broadcasted_iota(jnp.int32, (64, LANES), 1)
    pair = jnp.where(lane64 == 0, rows, pltpu.roll(rows, HALF, 1))
    ds_out[...] = pair.T[0:2, :]
    acc = jnp.zeros((8, LANES), F32)
    for t in range(4):
        tile = scales[t // 2][2][8 * (t % 2) : 8 * (t % 2) + 8]
        acc = jnp.where(lane8 == 2 * t, tile, acc)
        acc = jnp.where(lane8 == 2 * t + 1, pltpu.roll(tile, HALF, 1), acc)
    for g in range(2):
        gs_out[g, :, :] = acc[4 * g : 4 * g + 4, 0:7]

    for h in range(2):
        back = ways(h)[1][1], ways(h)[0][1]
        for w, _, _, rest in ways(h):
            block = G.at[core, h, back[w], rest]
            wait_bytes(block, recv.at[A2B + 2 * h + w])
            remote(block, block, SC + h, SC + h, sibling, fsdp).start()
    for h in range(2):
        far = (along[h][0] + 2) % 4
        for w, _, on, _ in ways(h):
            block = G.at[core, h, far, on]
            wait_bytes(block, recv.at[A2R + 2 * h + w])
            remote(block, block, SC + h, SC + h, sibling, fsdp).start()
    for h in range(2):
        wait_bytes(G.at[1 - core, h], recv.at[SC + h])
        for z2 in range(2):
            zh_ = 2 * h + z2
            for x_ in range(NX):
                gu_tiles = []
                for y_ in range(NY):
                    e1, e2 = (x_, y_) if h == 0 else (y_, x_)
                    col = ((zh_ * NX + x_) * NY + y_) * LANES
                    wide = []
                    for c in range(2):
                        for k in range(2):
                            row = 32 * c + 16 * k
                            dn_out[row : row + 16, col : col + LANES] = G[c, h, e1, e2, z2, k]
                        tile = G[c, h, e1, e2, z2, 2].astype(F32)
                        wide += [tile[0:8], tile[8:16]]
                    gu_tiles.append(wide)
                for yp in range(NY // 2):
                    even, odd = gu_tiles[2 * yp], gu_tiles[2 * yp + 1]
                    odd = pltpu.roll(jnp.concatenate(odd, axis=1), HALF, 1)
                    joined = jnp.where(lane8 < HALF, even[3], odd[:, 0:128])
                    full = jnp.concatenate(even[:3] + [joined, odd[:, 128:512]], axis=1)
                    col = ((zh_ * NX + x_) * NY + 2 * yp) * GUCOLS
                    for g in range(2):
                        gu_out[g, :, col : col + 2 * GUCOLS] = full[4 * g : 4 * g + 4].astype(BF)

    for h in range(2):
        wait_bytes(S.at[h, pl.ds(0, 3)], send.at[P1B + h])
        wait_bytes(R2.at[h, pl.ds(0, 7)], send.at[P2 + h])
        wait_bytes(G.at[core, h, 0, pl.ds(0, 3)], send.at[A1 + h])
        wait_bytes(G.at[core, h, pl.ds(0, 3)], send.at[A2A + h])
        wait_bytes(G.at[core, h], send.at[SC + h])
    wait_bytes(D.at[core], send.at[SDS])

    @pl.when(zl < OWN)
    def _():
        wait_bytes(R3.at[pl.ds(0, 22)], send.at[Z3])
        wait_bytes(R3.at[pl.ds(0, 15)], send.at[Z0])
        wait_bytes(D.at[core], send.at[SD])

    @pl.when(zl >= OWN)
    def _():
        wait_bytes(R3.at[pl.ds(0, 24)], send.at[Z3])


def place(*refs):
    n = (len(refs) - 1) // 2
    copies = [pltpu.make_async_copy(refs[i], refs[n + i], refs[-1].at[i]) for i in range(n)]
    for copy in copies:
        copy.start()
    for copy in copies:
        copy.wait()


def per_device(gu_pseudo, gu_master, gu_moment, down_pseudo, down_master, down_moment):
    shapes = (
        jax.ShapeDtypeStruct(gu_pseudo.shape[2:], BF),
        jax.ShapeDtypeStruct(down_pseudo.shape[2:], BF),
        jax.ShapeDtypeStruct(gu_master.shape, F32),
        jax.ShapeDtypeStruct(down_master.shape, F32),
        jax.ShapeDtypeStruct(gu_master.shape, F32),
        jax.ShapeDtypeStruct(down_master.shape, F32),
        jax.ShapeDtypeStruct(gu_master.shape[:2] + (7,), F32),
        jax.ShapeDtypeStruct((2, down_master.shape[0]), F32),
    )
    operands = [
        pltpu.with_memory_space_constraint(a, pltpu.HBM)
        for a in (gu_pseudo, gu_master, gu_moment, down_pseudo, down_master, down_moment)
    ]
    vmem = pl.BlockSpec(memory_space=pltpu.VMEM)
    hbm = pl.BlockSpec(memory_space=pl.ANY)
    results = pl.pallas_call(
        kernel,
        out_shape=shapes,
        in_specs=[hbm] * 6,
        out_specs=[vmem] * 8,
        scratch_shapes=[
            pltpu.VMEM(gu_pseudo.shape, BF),
            pltpu.VMEM(down_pseudo.shape, BF),
            pltpu.VMEM(gu_master.shape, F32),
            pltpu.VMEM(gu_master.shape, F32),
            pltpu.VMEM(down_master.shape, F32),
            pltpu.VMEM(down_master.shape, F32),
            pltpu.VMEM((2, 4, 4, 2, 2, 48, LANES), BF),
            pltpu.VMEM((2, 2, 2, 2, 2, 48, LANES), BF),
            pltpu.VMEM((2, 2, 4, 2, 2, 48, LANES), BF),
            pltpu.VMEM((2, 4, 2, 2, 48, LANES), BF),
            pltpu.VMEM((2, 8, 2, 48, LANES), BF),
            pltpu.VMEM((4, OWN, 2, 16, LANES), BF),
            pltpu.VMEM((32, 16, LANES), BF),
            pltpu.VMEM((2, OWN, 2, 16, LANES), F32),
            pltpu.VMEM((2, 2, 4, 4, 2, OWN, 16, LANES), BF),
            pltpu.VMEM((2, OWN, 16, LANES), F32),
            pltpu.VMEM((2, OWN, 16, LANES), F32),
            pltpu.SemaphoreType.DMA((NSEM,)),
            pltpu.SemaphoreType.DMA((NSEM,)),
            pltpu.SemaphoreType.DMA((6,)),
        ],
        compiler_params=pltpu.CompilerParams(
            collective_id=0, has_side_effects=True, vmem_limit_bytes=40 * MIB
        ),
    )(*operands)
    results = pl.pallas_call(
        place,
        out_shape=shapes,
        in_specs=[vmem] * 8,
        out_specs=[hbm] * 8,
        scratch_shapes=[pltpu.SemaphoreType.DMA((8,))],
        compiler_params=pltpu.CompilerParams(vmem_limit_bytes=40 * MIB),
    )(*results)
    return tuple(results[:7]) + (results[7].T,)


def solution(mesh):
    in_specs = (
        P("rep", "fsdp", None, None, None),
        P(None, None, "fsdp"),
        P(None, None, "fsdp"),
        P("rep", "fsdp", None, None),
        P(None, "fsdp"),
        P(None, "fsdp"),
    )
    out_specs = (
        P(),
        P(),
        P(None, None, "fsdp"),
        P(None, "fsdp"),
        P(None, None, "fsdp"),
        P(None, "fsdp"),
        P(None, None, "fsdp"),
        P(None, "fsdp"),
    )
    return jax.shard_map(
        per_device, mesh=mesh, in_specs=in_specs, out_specs=out_specs, check_vma=False
    )
```

```python
import jax
import jax.numpy as jnp
from jax import lax
from jax.experimental import pallas as pl
from jax.experimental.pallas import tpu as pltpu
from jax.sharding import PartitionSpec as P

NX = 4
NY = 4
ZH = 4
ZL = 4
LANES = 128
HALF = 64
GUCOLS = 448
OWN = 3
BF = jnp.bfloat16
F32 = jnp.float32
MIB = 1024 * 1024

P1A, P1B, P2, Z3, Z0, SD, SDS, A1, A2, SC = 0, 8, 12, 16, 17, 19, 20, 21, 25, 37
NSEM = 41


def kernel(
    gu_ref, gm_ref, gmo_ref, dn_ref, dm_ref, dmo_ref,
    gu_out, dn_out, gm_out, dm_out, gmo_out, dmo_out, gs_out, ds_out,
    gu_in, dn_in, gm_in, gmo_in, dm_in, dmo_in,
    S, RA, R1, PS, R2, Q, R3, D, G, M, MO, send, recv, local, line,
):
    rep = lax.axis_index("rep")
    fsdp = lax.axis_index("fsdp")
    zl, core = rep // 2, rep % 2
    zh, x, y = fsdp // (NX * NY), (fsdp // NY) % NX, fsdp % NY
    z = zh * ZL + zl
    along = ((x, y), (y, x))
    sibling = zl * 2 + (1 - core)
    pairs = [(g, h) for g in range(2) for h in range(2)]

    def fs(zh_, x_, y_):
        return (zh_ * NX + x_) * NY + y_

    def first_peer(h, d):
        return fs(zh, d, y) if h == 0 else fs(zh, x, d)

    def second_peer(h, d):
        return fs(zh, x, d) if h == 0 else fs(zh, d, y)

    def on_line(oz):
        return (oz % ZL) * 2 + core, fs(oz // ZL, x, y)

    def remote(src, dst, out, sem, rep_, fsdp_):
        return pltpu.make_async_remote_copy(
            src_ref=src, dst_ref=dst, send_sem=send.at[out], recv_sem=recv.at[sem],
            device_id={"rep": rep_, "fsdp": fsdp_}, device_id_type=pl.DeviceIdType.MESH,
        )

    def wait_bytes(ref, sem):
        pltpu.make_async_copy(ref, ref, sem).wait()

    loads = [
        pltpu.make_async_copy(src, dst, local.at[i])
        for i, (src, dst) in enumerate(
            (
                (dn_ref, dn_in), (gu_ref, gu_in), (dm_ref, dm_in), (dmo_ref, dmo_in),
                (gm_ref, gm_in), (gmo_ref, gmo_in),
            )
        )
    ]
    for load in loads:
        load.start()

    def signal(sem, rep_, fsdp_):
        pl.semaphore_signal(
            sem, inc=1, device_id={"rep": rep_, "fsdp": fsdp_}, device_id_type=pl.DeviceIdType.MESH
        )

    barrier = pltpu.get_barrier_semaphore()
    for r in (rep, sibling):
        for d in (2, 1, 3):
            signal(barrier, r, fs(zh, (x + d) % 4, y))
            signal(barrier, r, fs(zh, x, (y + d) % 4))
    for d in (1, 15):
        signal(barrier, *on_line((z + d) % 16))
    signal(barrier, sibling, fsdp)

    lane = lax.broadcasted_iota(jnp.int32, (8, 512), 1)
    lane8 = lax.broadcasted_iota(jnp.int32, (8, LANES), 1)

    def arrange(g):
        for h in range(2):
            zh_ = 2 * h + g
            for x_ in range(NX):
                for y_ in range(NY):
                    d1, d2 = (x_, y_) if h == 0 else (y_, x_)
                    col = ((zh_ * NX + x_) * NY + y_) * LANES
                    for c in range(2):
                        S[g, h, d1, d2, c, 0:32, :] = dn_in[0, 0, 32 * c : 32 * c + 32, col : col + LANES]
                for yp in range(NY // 2):
                    col = ((zh_ * NX + x_) * NY + 2 * yp) * GUCOLS
                    both = jnp.concatenate(
                        [gu_in[0, 0, i, :, col : col + 2 * GUCOLS].astype(F32) for i in range(2)], axis=0
                    )
                    odd = pltpu.roll(both[:, 384:896], 512 - HALF, 1)
                    for o, part in enumerate((both[:, 0:512], odd)):
                        part = jnp.where(lane < GUCOLS, part, 0.0)
                        y_ = 2 * yp + o
                        d1, d2 = (x_, y_) if h == 0 else (y_, x_)
                        for c in range(2):
                            two = jnp.concatenate(
                                [part[:, 256 * c : 256 * c + 128], part[:, 256 * c + 128 : 256 * c + 256]], axis=0
                            )
                            S[g, h, d1, d2, c, 32:48, :] = two.astype(BF)

    def ways(h):
        mine = along[h][0]
        return (
            (0, (mine + 1) % 4, pl.ds(0, 2), pl.ds(2, 2)),
            (1, (mine + 3) % 4, pl.ds(2, 2), pl.ds(0, 2)),
        )

    def first_axis(g):
        for h in range(2):
            far = (along[h][0] + 2) % 4
            for w, near, on, _ in ways(h):
                remote(
                    S.at[g, h, far, on], RA.at[g, h, w], P1B + 2 * g + h, P1A + 4 * g + 2 * h + w,
                    rep, first_peer(h, near),
                ).start()
        for h in range(2):
            for w, near, _, rest in ways(h):
                sem = P1B + 2 * g + h
                remote(S.at[g, h, near, rest], R1.at[g, h, w, rest], sem, sem, rep, first_peer(h, near)).start()

    def pass_on(g):
        for h in range(2):
            for w, near, on, _ in ways(h):
                wait_bytes(RA.at[g, h, w], recv.at[P1A + 4 * g + 2 * h + w])
                S[g, h, near, on] = (S[g, h, near, on].astype(F32) + RA[g, h, w].astype(F32)).astype(BF)
                sem = P1B + 2 * g + h
                remote(S.at[g, h, near, on], R1.at[g, h, w, on], sem, sem, rep, first_peer(h, near)).start()

    def second_axis(g):
        for h in range(2):
            mine, other = along[h]
            sem = P2 + 2 * g + h
            wait_bytes(R1.at[g, h], recv.at[P1B + 2 * g + h])
            for d in (2, 1, 3, 0):
                dest = (other + d) % 4
                acc = S[g, h, mine, dest].astype(F32) + R1[g, h, 0, dest].astype(F32)
                acc = acc + R1[g, h, 1, dest].astype(F32)
                PS[g, h, dest] = acc.astype(BF)
                if d:
                    to = second_peer(h, dest)
                    slot = R2.at[g, h, 2 * (d - 1) + core]
                    remote(PS.at[g, h, dest, core], slot, sem, sem, rep, to).start()
                    remote(PS.at[g, h, dest, 1 - core], slot, sem, sem, sibling, to).start()
                else:
                    remote(PS.at[g, h, dest, 1 - core], R2.at[g, h, 6 + core], sem, sem, sibling, fsdp).start()
                    R2[g, h, 6 + core] = PS[g, h, dest, core]

    def to_owners(g):
        for h in range(2):
            to = 2 * h + g
            wait_bytes(R2.at[g, h, pl.ds(0, 7)], recv.at[P2 + 2 * g + h])
            for c in range(2):
                acc = R2[g, h, c].astype(F32)
                for i in range(1, 4):
                    acc = acc + R2[g, h, 2 * i + c].astype(F32)
                acc = acc.astype(BF).reshape(OWN, 16, LANES)
                for k in range(OWN):
                    Q[to, k, c] = acc[k]
            for k in range(OWN):
                copy = remote(Q.at[to, k], R3.at[pl.ds(2 * z, 2)], Z3, Z3, 2 * k + core, fs(to, x, y))
                pl.when(jnp.logical_or(zh != to, zl != k))(copy.start)

    loads[0].wait()
    loads[1].wait()
    arrange(0)
    pl.semaphore_wait(barrier, 15)
    first_axis(0)
    arrange(1)
    first_axis(1)

    for i, d in enumerate((1, 2, 4)):
        signal(line.at[i], *on_line((z + d) % 16))
        signal(line.at[i], *on_line((z + 16 - d) % 16))
        pl.semaphore_wait(line.at[i], 2)
        if i == 0:
            for load in loads[2:]:
                load.wait()
            for g_ref, d_ref, out in ((gm_in, dm_in, M), (gmo_in, dmo_in, MO)):
                for c in range(2):
                    for k in range(2):
                        row = 32 * c + 16 * k
                        out[c, k] = d_ref[row : row + 16, :]
                for j in range(2):
                    for t in range(4):
                        row = 8 * (t % 2) + 4 * j
                        if t < 3:
                            out[t // 2, 2, row : row + 4, :] = g_ref[j, :, 128 * t : 128 * t + 128]
                        else:
                            out[1, 2, row : row + 4, :] = jnp.concatenate(
                                [g_ref[j, :, 384:448], jnp.zeros((4, HALF), F32)], axis=1
                            )
        if i == 1:
            pass_on(0)
    pass_on(1)
    second_axis(0)
    second_axis(1)
    to_owners(0)
    to_owners(1)

    hh, gg = zh // 2, zh % 2
    d1 = jnp.where(hh == 0, x, y)
    d2 = jnp.where(hh == 0, y, x)

    @pl.when(zl < OWN)
    def _():
        R3[pl.ds(2 * z, 2)] = Q[zh, zl]
        wait_bytes(R3.at[pl.ds(0, 30)], recv.at[Z3])
        largest = jnp.zeros((16, LANES), F32)
        total = jnp.zeros((16, LANES), F32)
        for r in range(8):
            part = R3[r].astype(F32)
            for k in range(1, 4):
                part = part + R3[8 * k + r].astype(F32)
            largest = jnp.maximum(largest, jnp.abs(part))
            total = total + part
        delta = total / 8
        moment = 0.9 * MO[core, zl] + delta
        master = M[core, zl] - 0.7 * (delta + 0.9 * moment)
        mine = G.at[core, gg, hh, d1, d2, zl]
        mine[...] = master.astype(BF)

        def spread(k, carry):
            oz = (z + 8 + jnp.where(k % 2 == 0, k // 2, 16 - (k + 1) // 2)) % 16
            remote(mine, mine, Z0, Z0 + gg, *on_line(oz)).start()
            return carry

        lax.fori_loop(0, 15, spread, 0)
        low = lax.broadcasted_iota(jnp.int32, (16, LANES), 1) < HALF
        low_max = jnp.max(jnp.where(low, largest, 0.0), axis=1, keepdims=True)
        high_max = jnp.max(jnp.where(low, 0.0, largest), axis=1, keepdims=True)
        D[core, zl, 0] = delta
        D[core, zl, 1] = jnp.where(low, low_max, high_max) + 1e-6
        for k in range(1, 4):
            block = D.at[core, zl]
            remote(block, block, SD, SD, ((zl + k) % ZL) * 2 + core, fsdp).start()

    def gather_second(g):
        owner = jnp.logical_and(zl < OWN, gg == g)

        @pl.when(owner)
        def _():
            wait_bytes(R3.at[pl.ds(0, 5)], recv.at[Z0 + g])

        @pl.when(jnp.logical_not(owner))
        def _():
            wait_bytes(R3.at[pl.ds(0, 6)], recv.at[Z0 + g])

        for h in range(2):
            mine, other = along[h]
            sem = A1 + 2 * g + h
            for d in (2, 1, 3):
                block = G.at[core, g, h, mine, other]
                remote(block, block, sem, sem, rep, second_peer(h, (other + d) % 4)).start()

    def to_sibling(g, h, d):
        block = G.at[core, g, h, d]
        remote(block, block, SC + 2 * g + h, SC + 2 * g + h, sibling, fsdp).start()

    def gather_first(g):
        for h in range(2):
            mine, other = along[h]
            wait_bytes(G.at[core, g, h, mine, pl.ds(0, 3)], recv.at[A1 + 2 * g + h])
            for d in (2, 1, 3):
                block = G.at[core, g, h, mine]
                remote(
                    block, block, A2 + 6 * g + 3 * h, A2 + 6 * g + 3 * h + d - 1,
                    rep, first_peer(h, (mine + d) % 4),
                ).start()
            to_sibling(g, h, mine)

    def share(g):
        for d in (1, 3, 2):
            for h in range(2):
                source = (along[h][0] + 4 - d) % 4
                wait_bytes(G.at[core, g, h, source], recv.at[A2 + 6 * g + 3 * h + d - 1])
                to_sibling(g, h, source)

    gather_second(0)
    gather_second(1)
    gather_first(0)

    @pl.when(zl < OWN)
    def _():
        wait_bytes(D.at[core, pl.ds(0, 2)], recv.at[SD])

    @pl.when(zl >= OWN)
    def _():
        wait_bytes(D.at[core], recv.at[SD])

    remote(D.at[core], D.at[core], SDS, SDS, sibling, fsdp).start()

    gather_first(1)
    share(0)

    wait_bytes(D.at[1 - core], recv.at[SDS])
    state = ([], [], [])
    for c in range(2):
        for k in range(OWN):
            moment = 0.9 * MO[c, k] + D[c, k, 0]
            state[0].append(moment)
            state[1].append(M[c, k] - 0.7 * (D[c, k, 0] + 0.9 * moment))
            state[2].append(D[c, k, 1])
    moments, masters, scales = ([s[0:3], s[3:6]] for s in state)
    for tiles, d_out, g_out in ((moments, dmo_out, gmo_out), (masters, dm_out, gm_out)):
        for c in range(2):
            for k in range(2):
                row = 32 * c + 16 * k
                d_out[row : row + 16, :] = tiles[c][k]
        for j in range(2):
            for t in range(4):
                row = 8 * (t % 2) + 4 * j
                width = 128 if t < 3 else 64
                g_out[j, :, 128 * t : 128 * t + width] = tiles[t // 2][2][row : row + 4, :width]
    rows = jnp.concatenate([scales[c][k] for c in range(2) for k in range(2)], axis=0)
    lane64 = lax.broadcasted_iota(jnp.int32, (64, LANES), 1)
    pair = jnp.where(lane64 == 0, rows, pltpu.roll(rows, HALF, 1))
    ds_out[...] = pair.T[0:2, :]
    acc = jnp.zeros((8, LANES), F32)
    for t in range(4):
        tile = scales[t // 2][2][8 * (t % 2) : 8 * (t % 2) + 8]
        acc = jnp.where(lane8 == 2 * t, tile, acc)
        acc = jnp.where(lane8 == 2 * t + 1, pltpu.roll(tile, HALF, 1), acc)
    for j in range(2):
        gs_out[j, :, :] = acc[4 * j : 4 * j + 4, 0:7]

    def write(g, h):
        zh_ = 2 * h + g
        wait_bytes(G.at[1 - core, g, h], recv.at[SC + 2 * g + h])
        for x_ in range(NX):
            gu_tiles = []
            for y_ in range(NY):
                e1, e2 = (x_, y_) if h == 0 else (y_, x_)
                col = ((zh_ * NX + x_) * NY + y_) * LANES
                wide = []
                for c in range(2):
                    for k in range(2):
                        row = 32 * c + 16 * k
                        dn_out[row : row + 16, col : col + LANES] = G[c, g, h, e1, e2, k]
                    tile = G[c, g, h, e1, e2, 2].astype(F32)
                    wide += [tile[0:8], tile[8:16]]
                gu_tiles.append(wide)
            for yp in range(NY // 2):
                even, odd = gu_tiles[2 * yp], gu_tiles[2 * yp + 1]
                odd = pltpu.roll(jnp.concatenate(odd, axis=1), HALF, 1)
                joined = jnp.where(lane8 < HALF, even[3], odd[:, 0:128])
                full = jnp.concatenate(even[:3] + [joined, odd[:, 128:512]], axis=1)
                col = ((zh_ * NX + x_) * NY + 2 * yp) * GUCOLS
                for j in range(2):
                    gu_out[j, :, col : col + 2 * GUCOLS] = full[4 * j : 4 * j + 4].astype(BF)

    write(0, 0)
    write(0, 1)
    share(1)
    write(1, 0)
    write(1, 1)

    for g, h in pairs:
        i = 2 * g + h
        wait_bytes(S.at[g, h, pl.ds(0, 3)], send.at[P1B + i])
        wait_bytes(R2.at[g, h, pl.ds(0, 7)], send.at[P2 + i])
        wait_bytes(G.at[core, g, h, 0, pl.ds(0, 3)], send.at[A1 + i])
        wait_bytes(G.at[core, g, h, pl.ds(0, 3)], send.at[A2 + 3 * i])
        wait_bytes(G.at[core, g, h], send.at[SC + i])
    wait_bytes(D.at[core], send.at[SDS])

    @pl.when(zl < OWN)
    def _():
        wait_bytes(R3.at[pl.ds(0, 22)], send.at[Z3])
        wait_bytes(R3.at[pl.ds(0, 15)], send.at[Z0])
        wait_bytes(D.at[core], send.at[SD])

    @pl.when(zl >= OWN)
    def _():
        wait_bytes(R3.at[pl.ds(0, 24)], send.at[Z3])


def place(*refs):
    n = (len(refs) - 1) // 2
    copies = [pltpu.make_async_copy(refs[i], refs[n + i], refs[-1].at[i]) for i in range(n)]
    for copy in copies:
        copy.start()
    for copy in copies:
        copy.wait()


def per_device(gu_pseudo, gu_master, gu_moment, down_pseudo, down_master, down_moment):
    shapes = (
        jax.ShapeDtypeStruct(gu_pseudo.shape[2:], BF),
        jax.ShapeDtypeStruct(down_pseudo.shape[2:], BF),
        jax.ShapeDtypeStruct(gu_master.shape, F32),
        jax.ShapeDtypeStruct(down_master.shape, F32),
        jax.ShapeDtypeStruct(gu_master.shape, F32),
        jax.ShapeDtypeStruct(down_master.shape, F32),
        jax.ShapeDtypeStruct(gu_master.shape[:2] + (7,), F32),
        jax.ShapeDtypeStruct((2, down_master.shape[0]), F32),
    )
    operands = [
        pltpu.with_memory_space_constraint(a, pltpu.HBM)
        for a in (gu_pseudo, gu_master, gu_moment, down_pseudo, down_master, down_moment)
    ]
    vmem = pl.BlockSpec(memory_space=pltpu.VMEM)
    hbm = pl.BlockSpec(memory_space=pl.ANY)
    results = pl.pallas_call(
        kernel,
        out_shape=shapes,
        in_specs=[hbm] * 6,
        out_specs=[vmem] * 8,
        scratch_shapes=[
            pltpu.VMEM(gu_pseudo.shape, BF),
            pltpu.VMEM(down_pseudo.shape, BF),
            pltpu.VMEM(gu_master.shape, F32),
            pltpu.VMEM(gu_master.shape, F32),
            pltpu.VMEM(down_master.shape, F32),
            pltpu.VMEM(down_master.shape, F32),
            pltpu.VMEM((2, 2, 4, 4, 2, 48, LANES), BF),
            pltpu.VMEM((2, 2, 2, 2, 2, 48, LANES), BF),
            pltpu.VMEM((2, 2, 2, 4, 2, 48, LANES), BF),
            pltpu.VMEM((2, 2, 4, 2, 48, LANES), BF),
            pltpu.VMEM((2, 2, 8, 48, LANES), BF),
            pltpu.VMEM((4, OWN, 2, 16, LANES), BF),
            pltpu.VMEM((32, 16, LANES), BF),
            pltpu.VMEM((2, OWN, 2, 16, LANES), F32),
            pltpu.VMEM((2, 2, 2, 4, 4, OWN, 16, LANES), BF),
            pltpu.VMEM((2, OWN, 16, LANES), F32),
            pltpu.VMEM((2, OWN, 16, LANES), F32),
            pltpu.SemaphoreType.DMA((NSEM,)),
            pltpu.SemaphoreType.DMA((NSEM,)),
            pltpu.SemaphoreType.DMA((6,)),
            pltpu.SemaphoreType.REGULAR((3,)),
        ],
        compiler_params=pltpu.CompilerParams(
            collective_id=0, has_side_effects=True, vmem_limit_bytes=40 * MIB
        ),
    )(*operands)
    results = pl.pallas_call(
        place,
        out_shape=shapes,
        in_specs=[vmem] * 8,
        out_specs=[hbm] * 8,
        scratch_shapes=[pltpu.SemaphoreType.DMA((8,))],
        compiler_params=pltpu.CompilerParams(vmem_limit_bytes=40 * MIB),
    )(*results)
    return tuple(results[:7]) + (results[7].T,)


def solution(mesh):
    in_specs = (
        P("rep", "fsdp", None, None, None),
        P(None, None, "fsdp"),
        P(None, None, "fsdp"),
        P("rep", "fsdp", None, None),
        P(None, "fsdp"),
        P(None, "fsdp"),
    )
    out_specs = (
        P(),
        P(),
        P(None, None, "fsdp"),
        P(None, "fsdp"),
        P(None, None, "fsdp"),
        P(None, "fsdp"),
        P(None, None, "fsdp"),
        P(None, "fsdp"),
    )
    return jax.shard_map(
        per_device, mesh=mesh, in_specs=in_specs, out_specs=out_specs, check_vma=False
    )
```

```python
import jax
import jax.numpy as jnp
from jax import lax
from jax.experimental import pallas as pl
from jax.experimental.pallas import tpu as pltpu
from jax.sharding import PartitionSpec as P

NX = 4
NY = 4
ZH = 4
ZL = 4
LANES = 128
HALF = 64
GUCOLS = 448
OWN = 3
SHARD = ((0, 2), (1, 3))
OWNER = (0, 2)
BF = jnp.bfloat16
F32 = jnp.float32
MIB = 1024 * 1024

P1A, P1B, P2, Z3, Z0, SD, SDS, A1, A2, SC = 0, 8, 12, 16, 17, 19, 20, 21, 25, 37
NSEM = 41


def kernel(
    gu_ref, gm_ref, gmo_ref, dn_ref, dm_ref, dmo_ref,
    gu_out, dn_out, gm_out, dm_out, gmo_out, dmo_out, gs_out, ds_out,
    gu_in, dn_in, gm_in, gmo_in, dm_in, dmo_in,
    S, RA, R1, PS, R2, Q, R3, D, G, M, MO, send, recv, local, line,
):
    rep = lax.axis_index("rep")
    fsdp = lax.axis_index("fsdp")
    zl, core = rep // 2, rep % 2
    zh, x, y = fsdp // (NX * NY), (fsdp // NY) % NX, fsdp % NY
    z = zh * ZL + zl
    along = ((x, y), (y, x))
    sibling = zl * 2 + (1 - core)
    owner = zl == OWNER[0] + core * (OWNER[1] - OWNER[0])
    pairs = [(g, h) for g in range(2) for h in range(2)]

    def fs(zh_, x_, y_):
        return (zh_ * NX + x_) * NY + y_

    def first_peer(h, d):
        return fs(zh, d, y) if h == 0 else fs(zh, x, d)

    def second_peer(h, d):
        return fs(zh, x, d) if h == 0 else fs(zh, d, y)

    def on_line(oz):
        return (oz % ZL) * 2 + core, fs(oz // ZL, x, y)

    def remote(src, dst, out, sem, rep_, fsdp_):
        return pltpu.make_async_remote_copy(
            src_ref=src, dst_ref=dst, send_sem=send.at[out], recv_sem=recv.at[sem],
            device_id={"rep": rep_, "fsdp": fsdp_}, device_id_type=pl.DeviceIdType.MESH,
        )

    def wait_bytes(ref, sem):
        pltpu.make_async_copy(ref, ref, sem).wait()

    loads = [
        pltpu.make_async_copy(src, dst, local.at[i])
        for i, (src, dst) in enumerate(
            (
                (dn_ref, dn_in), (gu_ref, gu_in), (dm_ref, dm_in), (dmo_ref, dmo_in),
                (gm_ref, gm_in), (gmo_ref, gmo_in),
            )
        )
    ]
    for load in loads:
        load.start()

    def signal(sem, rep_, fsdp_):
        pl.semaphore_signal(
            sem, inc=1, device_id={"rep": rep_, "fsdp": fsdp_}, device_id_type=pl.DeviceIdType.MESH
        )

    near = [
        (rep, fs(zh, (x + 1) % 4, y)), (rep, fs(zh, (x + 3) % 4, y)),
        (rep, fs(zh, x, (y + 1) % 4)), (rep, fs(zh, x, (y + 3) % 4)),
    ]
    barrier = pltpu.get_barrier_semaphore()
    for peer in near + [(sibling, fsdp), on_line((z + 1) % 16), on_line((z + 15) % 16)]:
        signal(barrier, *peer)

    rounds = (
        near + [on_line((z + 1) % 16), on_line((z + 15) % 16)],
        [on_line((z + 2) % 16), on_line((z + 14) % 16)],
        [on_line((z + 4) % 16), on_line((z + 12) % 16)],
        [(sibling, fsdp)],
    )

    def tell(i):
        for peer in rounds[i]:
            signal(line.at[i], *peer)

    def hear(i):
        pl.semaphore_wait(line.at[i], len(rounds[i]))

    lane = lax.broadcasted_iota(jnp.int32, (8, 512), 1)
    lane8 = lax.broadcasted_iota(jnp.int32, (8, LANES), 1)

    def arrange(g):
        for h in range(2):
            zh_ = SHARD[g][h]
            for x_ in range(NX):
                for y_ in range(NY):
                    d1, d2 = (x_, y_) if h == 0 else (y_, x_)
                    col = ((zh_ * NX + x_) * NY + y_) * LANES
                    for c in range(2):
                        S[g, h, d1, d2, c, 0:32, :] = dn_in[0, 0, 32 * c : 32 * c + 32, col : col + LANES]
                for yp in range(NY // 2):
                    col = ((zh_ * NX + x_) * NY + 2 * yp) * GUCOLS
                    both = jnp.concatenate(
                        [gu_in[0, 0, i, :, col : col + 2 * GUCOLS].astype(F32) for i in range(2)], axis=0
                    )
                    odd = pltpu.roll(both[:, 384:896], 512 - HALF, 1)
                    for o, part in enumerate((both[:, 0:512], odd)):
                        part = jnp.where(lane < GUCOLS, part, 0.0)
                        y_ = 2 * yp + o
                        d1, d2 = (x_, y_) if h == 0 else (y_, x_)
                        for c in range(2):
                            two = jnp.concatenate(
                                [part[:, 256 * c : 256 * c + 128], part[:, 256 * c + 128 : 256 * c + 256]], axis=0
                            )
                            S[g, h, d1, d2, c, 32:48, :] = two.astype(BF)

    def ways(h):
        mine = along[h][0]
        return (
            (0, (mine + 1) % 4, pl.ds(0, 2), pl.ds(2, 2)),
            (1, (mine + 3) % 4, pl.ds(2, 2), pl.ds(0, 2)),
        )

    def ahead(g):
        for h in range(2):
            far = (along[h][0] + 2) % 4
            for w, near, on, _ in ways(h):
                remote(
                    S.at[g, h, far, on], RA.at[g, h, w], P1B + 2 * g + h, P1A + 4 * g + 2 * h + w,
                    rep, first_peer(h, near),
                ).start()

    def rest_of(g):
        for h in range(2):
            for w, near, _, rest in ways(h):
                sem = P1B + 2 * g + h
                remote(S.at[g, h, near, rest], R1.at[g, h, w, rest], sem, sem, rep, first_peer(h, near)).start()

    def pass_on(g):
        for h in range(2):
            for w, near, on, _ in ways(h):
                wait_bytes(RA.at[g, h, w], recv.at[P1A + 4 * g + 2 * h + w])
                S[g, h, near, on] = (S[g, h, near, on].astype(F32) + RA[g, h, w].astype(F32)).astype(BF)
                sem = P1B + 2 * g + h
                remote(S.at[g, h, near, on], R1.at[g, h, w, on], sem, sem, rep, first_peer(h, near)).start()

    def second_axis(g):
        for h in range(2):
            mine, other = along[h]
            sem = P2 + 2 * g + h
            wait_bytes(R1.at[g, h], recv.at[P1B + 2 * g + h])
            for d in (2, 1, 3, 0):
                dest = (other + d) % 4
                acc = S[g, h, mine, dest].astype(F32) + R1[g, h, 0, dest].astype(F32)
                acc = acc + R1[g, h, 1, dest].astype(F32)
                PS[g, h, dest] = acc.astype(BF)
                if d:
                    remote(PS.at[g, h, dest], R2.at[g, h, d - 1], sem, sem, rep, second_peer(h, dest)).start()

    def to_owners(g):
        for h in range(2):
            to = SHARD[g][h]
            wait_bytes(R2.at[g, h], recv.at[P2 + 2 * g + h])
            acc = PS[g, h, along[h][1]].astype(F32)
            for i in range(3):
                acc = acc + R2[g, h, i].astype(F32)
            Q[to] = acc.astype(BF)
            for c in range(2):
                copy = remote(Q.at[to, c], R3.at[2 * z + core], Z3, Z3, 2 * OWNER[c] + c, fs(to, x, y))
                pl.when(jnp.logical_or(fsdp != fs(to, x, y), rep != 2 * OWNER[c] + c))(copy.start)

    loads[0].wait()
    loads[1].wait()
    arrange(0)
    pl.semaphore_wait(barrier, 7)
    ahead(0)
    arrange(1)
    ahead(1)
    rest_of(0)
    rest_of(1)
    tell(0)
    hear(0)
    tell(1)
    pass_on(0)
    pass_on(1)
    for load in loads[2:]:
        load.wait()
    for g_ref, d_ref, out in ((gm_in, dm_in, M), (gmo_in, dmo_in, MO)):
        for c in range(2):
            for k in range(2):
                row = 32 * c + 16 * k
                out[c, 16 * k : 16 * k + 16, :] = d_ref[row : row + 16, :]
        for j in range(2):
            for t in range(4):
                row = 8 * (t % 2) + 4 * j
                if t < 3:
                    out[t // 2, 32 + row : 36 + row, :] = g_ref[j, :, 128 * t : 128 * t + 128]
                else:
                    out[1, 32 + row : 36 + row, :] = jnp.concatenate(
                        [g_ref[j, :, 384:448], jnp.zeros((4, HALF), F32)], axis=1
                    )
    hear(1)
    tell(2)
    second_axis(0)
    second_axis(1)
    hear(2)
    tell(3)
    hear(3)
    to_owners(0)
    to_owners(1)

    hh, gg = zh // 2, zh % 2
    d1 = jnp.where(hh == 0, x, y)

    @pl.when(owner)
    def _():
        R3[2 * z + core] = Q[zh, core]
        wait_bytes(R3.at[pl.ds(0, 31)], recv.at[Z3])
        largest = jnp.zeros((48, LANES), F32)
        total = jnp.zeros((48, LANES), F32)
        for r in range(8):
            part = R3[r].astype(F32)
            for k in range(1, 4):
                part = part + R3[8 * k + r].astype(F32)
            largest = jnp.maximum(largest, jnp.abs(part))
            total = total + part
        delta = total / 8
        moment = 0.9 * MO[core] + delta
        master = M[core] - 0.7 * (delta + 0.9 * moment)
        mine = G.at[core, gg, hh, d1, 0]
        mine[...] = master.astype(BF)
        for k in (8, 7, 9, 6, 10, 5, 11, 4, 12, 3, 13, 2, 14, 1, 15):
            remote(mine, mine, Z0, Z0 + gg, *on_line((z + k) % 16)).start()
        low = lax.broadcasted_iota(jnp.int32, (48, LANES), 1) < HALF
        low_max = jnp.max(jnp.where(low, largest, 0.0), axis=1, keepdims=True)
        high_max = jnp.max(jnp.where(low, 0.0, largest), axis=1, keepdims=True)
        D[core, 0] = delta
        D[core, 1] = jnp.where(low, low_max, high_max) + 1e-6

    def gather_second(g):
        made = jnp.logical_and(owner, gg == g)

        @pl.when(made)
        def _():
            wait_bytes(R3.at[0], recv.at[Z0 + g])

        @pl.when(jnp.logical_not(made))
        def _():
            wait_bytes(R3.at[pl.ds(0, 2)], recv.at[Z0 + g])

        for h in range(2):
            mine, other = along[h]
            sem = A1 + 2 * g + h
            block = G.at[core, g, h, mine, 0]
            for d in (2, 1, 3):
                to = second_peer(h, (other + d) % 4)
                remote(block, G.at[core, g, h, mine, 4 - d], sem, sem, rep, to).start()
        for h in range(2):
            mine = along[h][0]
            block = G.at[core, g, h, mine, 0]
            for d in (2, 1, 3):
                to = first_peer(h, (mine + d) % 4)
                remote(block, block, A1 + 2 * g + h, A2 + 6 * g + 3 * h + d - 1, rep, to).start()

    def to_sibling(g, h, d):
        block = G.at[core, g, h, d]
        remote(block, block, SC + 2 * g + h, SC + 2 * g + h, sibling, fsdp).start()

    def gather_first(g):
        for h in range(2):
            mine, other = along[h]
            wait_bytes(G.at[core, g, h, mine, pl.ds(1, 3)], recv.at[A1 + 2 * g + h])
            for d in (2, 1, 3):
                block = G.at[core, g, h, mine, pl.ds(1, 3)]
                remote(
                    block, block, A2 + 6 * g + 3 * h, A2 + 6 * g + 3 * h + d - 1,
                    rep, first_peer(h, (mine + d) % 4),
                ).start()
            to_sibling(g, h, mine)

    def share(g):
        for d in (1, 3, 2):
            for h in range(2):
                source = (along[h][0] + 4 - d) % 4
                wait_bytes(G.at[core, g, h, source], recv.at[A2 + 6 * g + 3 * h + d - 1])
                to_sibling(g, h, source)

    gather_second(0)
    gather_second(1)

    @pl.when(owner)
    def _():
        for k in range(1, 4):
            block = D.at[core]
            remote(block, block, SD, SD, ((zl + k) % ZL) * 2 + core, fsdp).start()

    gather_first(0)

    gather_first(1)
    share(0)

    @pl.when(jnp.logical_not(owner))
    def _():
        wait_bytes(D.at[core], recv.at[SD])

    remote(D.at[core], D.at[core], SDS, SDS, sibling, fsdp).start()

    def write(g, h):
        zh_ = SHARD[g][h]
        wait_bytes(G.at[1 - core, g, h], recv.at[SC + 2 * g + h])
        for x_ in range(NX):
            gu_tiles = []
            for y_ in range(NY):
                e1, e2 = (x_, (y_ + 4 - y) % 4) if h == 0 else (y_, (x_ + 4 - x) % 4)
                col = ((zh_ * NX + x_) * NY + y_) * LANES
                wide = []
                for c in range(2):
                    for k in range(2):
                        row = 32 * c + 16 * k
                        dn_out[row : row + 16, col : col + LANES] = G[c, g, h, e1, e2, 16 * k : 16 * k + 16]
                    tile = G[c, g, h, e1, e2, 32:48].astype(F32)
                    wide += [tile[0:8], tile[8:16]]
                gu_tiles.append(wide)
            for yp in range(NY // 2):
                even, odd = gu_tiles[2 * yp], gu_tiles[2 * yp + 1]
                odd = pltpu.roll(jnp.concatenate(odd, axis=1), HALF, 1)
                joined = jnp.where(lane8 < HALF, even[3], odd[:, 0:128])
                full = jnp.concatenate(even[:3] + [joined, odd[:, 128:512]], axis=1)
                col = ((zh_ * NX + x_) * NY + 2 * yp) * GUCOLS
                for j in range(2):
                    gu_out[j, :, col : col + 2 * GUCOLS] = full[4 * j : 4 * j + 4].astype(BF)

    write(0, 0)
    write(0, 1)
    share(1)

    wait_bytes(D.at[1 - core], recv.at[SDS])
    moments, masters, scales = [], [], []
    for c in range(2):
        delta, scale = D[c, 0], D[c, 1]
        moment = 0.9 * MO[c] + delta
        master = M[c] - 0.7 * (delta + 0.9 * moment)
        for tiles, value in ((moments, moment), (masters, master), (scales, scale)):
            tiles.append([value[16 * k : 16 * k + 16] for k in range(OWN)])
    for tiles, d_out, g_out in ((moments, dmo_out, gmo_out), (masters, dm_out, gm_out)):
        for c in range(2):
            for k in range(2):
                row = 32 * c + 16 * k
                d_out[row : row + 16, :] = tiles[c][k]
        for j in range(2):
            for t in range(4):
                row = 8 * (t % 2) + 4 * j
                width = 128 if t < 3 else 64
                g_out[j, :, 128 * t : 128 * t + width] = tiles[t // 2][2][row : row + 4, :width]
    rows = jnp.concatenate([scales[c][k] for c in range(2) for k in range(2)], axis=0)
    lane64 = lax.broadcasted_iota(jnp.int32, (64, LANES), 1)
    pair = jnp.where(lane64 == 0, rows, pltpu.roll(rows, HALF, 1))
    ds_out[...] = pair.T[0:2, :]
    acc = jnp.zeros((8, LANES), F32)
    for t in range(4):
        tile = scales[t // 2][2][8 * (t % 2) : 8 * (t % 2) + 8]
        acc = jnp.where(lane8 == 2 * t, tile, acc)
        acc = jnp.where(lane8 == 2 * t + 1, pltpu.roll(tile, HALF, 1), acc)
    for j in range(2):
        gs_out[j, :, :] = acc[4 * j : 4 * j + 4, 0:7]

    write(1, 0)
    write(1, 1)

    for g, h in pairs:
        i = 2 * g + h
        wait_bytes(S.at[g, h, pl.ds(0, 3)], send.at[P1B + i])
        wait_bytes(R2.at[g, h], send.at[P2 + i])
        wait_bytes(R3.at[pl.ds(0, 6)], send.at[A1 + i])
        wait_bytes(R3.at[pl.ds(0, 9)], send.at[A2 + 3 * i])
        wait_bytes(G.at[core, g, h], send.at[SC + i])
    wait_bytes(D.at[core], send.at[SDS])

    @pl.when(owner)
    def _():
        wait_bytes(R3.at[pl.ds(0, 7)], send.at[Z3])
        wait_bytes(R3.at[pl.ds(0, 15)], send.at[Z0])
        wait_bytes(R3.at[pl.ds(0, 12)], send.at[SD])

    @pl.when(jnp.logical_not(owner))
    def _():
        wait_bytes(R3.at[pl.ds(0, 8)], send.at[Z3])


def place(*refs):
    n = (len(refs) - 1) // 2
    copies = [pltpu.make_async_copy(refs[i], refs[n + i], refs[-1].at[i]) for i in range(n)]
    for copy in copies:
        copy.start()
    for copy in copies:
        copy.wait()


def per_device(gu_pseudo, gu_master, gu_moment, down_pseudo, down_master, down_moment):
    shapes = (
        jax.ShapeDtypeStruct(gu_pseudo.shape[2:], BF),
        jax.ShapeDtypeStruct(down_pseudo.shape[2:], BF),
        jax.ShapeDtypeStruct(gu_master.shape, F32),
        jax.ShapeDtypeStruct(down_master.shape, F32),
        jax.ShapeDtypeStruct(gu_master.shape, F32),
        jax.ShapeDtypeStruct(down_master.shape, F32),
        jax.ShapeDtypeStruct(gu_master.shape[:2] + (7,), F32),
        jax.ShapeDtypeStruct((2, down_master.shape[0]), F32),
    )
    operands = [
        pltpu.with_memory_space_constraint(a, pltpu.HBM)
        for a in (gu_pseudo, gu_master, gu_moment, down_pseudo, down_master, down_moment)
    ]
    vmem = pl.BlockSpec(memory_space=pltpu.VMEM)
    hbm = pl.BlockSpec(memory_space=pl.ANY)
    results = pl.pallas_call(
        kernel,
        out_shape=shapes,
        in_specs=[hbm] * 6,
        out_specs=[vmem] * 8,
        scratch_shapes=[
            pltpu.VMEM(gu_pseudo.shape, BF),
            pltpu.VMEM(down_pseudo.shape, BF),
            pltpu.VMEM(gu_master.shape, F32),
            pltpu.VMEM(gu_master.shape, F32),
            pltpu.VMEM(down_master.shape, F32),
            pltpu.VMEM(down_master.shape, F32),
            pltpu.VMEM((2, 2, 4, 4, 2, 48, LANES), BF),
            pltpu.VMEM((2, 2, 2, 2, 2, 48, LANES), BF),
            pltpu.VMEM((2, 2, 2, 4, 2, 48, LANES), BF),
            pltpu.VMEM((2, 2, 4, 2, 48, LANES), BF),
            pltpu.VMEM((2, 2, 3, 2, 48, LANES), BF),
            pltpu.VMEM((4, 2, 48, LANES), BF),
            pltpu.VMEM((32, 48, LANES), BF),
            pltpu.VMEM((2, 2, 48, LANES), F32),
            pltpu.VMEM((2, 2, 2, 4, 4, 48, LANES), BF),
            pltpu.VMEM((2, 48, LANES), F32),
            pltpu.VMEM((2, 48, LANES), F32),
            pltpu.SemaphoreType.DMA((NSEM,)),
            pltpu.SemaphoreType.DMA((NSEM,)),
            pltpu.SemaphoreType.DMA((6,)),
            pltpu.SemaphoreType.REGULAR((4,)),
        ],
        compiler_params=pltpu.CompilerParams(
            collective_id=0, has_side_effects=True, vmem_limit_bytes=40 * MIB
        ),
    )(*operands)
    results = pl.pallas_call(
        place,
        out_shape=shapes,
        in_specs=[vmem] * 8,
        out_specs=[hbm] * 8,
        scratch_shapes=[pltpu.SemaphoreType.DMA((8,))],
        compiler_params=pltpu.CompilerParams(vmem_limit_bytes=40 * MIB),
    )(*results)
    return tuple(results[:7]) + (results[7].T,)


def solution(mesh):
    in_specs = (
        P("rep", "fsdp", None, None, None),
        P(None, None, "fsdp"),
        P(None, None, "fsdp"),
        P("rep", "fsdp", None, None),
        P(None, "fsdp"),
        P(None, "fsdp"),
    )
    out_specs = (
        P(),
        P(),
        P(None, None, "fsdp"),
        P(None, "fsdp"),
        P(None, None, "fsdp"),
        P(None, "fsdp"),
        P(None, None, "fsdp"),
        P(None, "fsdp"),
    )
    return jax.shard_map(
        per_device, mesh=mesh, in_specs=in_specs, out_specs=out_specs, check_vma=False
    )
```

```python
import jax
import jax.numpy as jnp
from jax import lax
from jax.experimental import pallas as pl
from jax.experimental.pallas import tpu as pltpu
from jax.sharding import PartitionSpec as P

NX = 4
NY = 4
ZH = 4
ZL = 4
LANES = 128
HALF = 64
GUCOLS = 448
OWN = 3
SHARD = ((0, 2), (1, 3))
OWNER = (2, 0)
BF = jnp.bfloat16
F32 = jnp.float32
MIB = 1024 * 1024

P1A, P1B, P2, Z3, Z0, SD, SDS, A1, A2, SC = 0, 8, 12, 16, 17, 19, 20, 21, 25, 37
NSEM = 41


def kernel(
    gu_ref, gm_ref, gmo_ref, dn_ref, dm_ref, dmo_ref,
    gu_out, dn_out, gm_out, dm_out, gmo_out, dmo_out, gs_out, ds_out,
    gu_in, dn_in, gm_in, gmo_in, dm_in, dmo_in,
    S, RA, R1, PS, R2, Q, R3, D, G, M, MO, send, recv, local, line,
):
    rep = lax.axis_index("rep")
    fsdp = lax.axis_index("fsdp")
    zl, core = rep // 2, rep % 2
    zh, x, y = fsdp // (NX * NY), (fsdp // NY) % NX, fsdp % NY
    z = zh * ZL + zl
    along = ((x, y), (y, x))
    sibling = zl * 2 + (1 - core)
    owner = zl == OWNER[0] + core * (OWNER[1] - OWNER[0])
    pairs = [(g, h) for g in range(2) for h in range(2)]

    def fs(zh_, x_, y_):
        return (zh_ * NX + x_) * NY + y_

    def first_peer(h, d):
        return fs(zh, d, y) if h == 0 else fs(zh, x, d)

    def second_peer(h, d):
        return fs(zh, x, d) if h == 0 else fs(zh, d, y)

    def on_line(oz):
        return (oz % ZL) * 2 + core, fs(oz // ZL, x, y)

    def remote(src, dst, out, sem, rep_, fsdp_):
        return pltpu.make_async_remote_copy(
            src_ref=src, dst_ref=dst, send_sem=send.at[out], recv_sem=recv.at[sem],
            device_id={"rep": rep_, "fsdp": fsdp_}, device_id_type=pl.DeviceIdType.MESH,
        )

    def wait_bytes(ref, sem):
        pltpu.make_async_copy(ref, ref, sem).wait()

    loads = [
        pltpu.make_async_copy(src, dst, local.at[i])
        for i, (src, dst) in enumerate(
            (
                (dn_ref, dn_in), (gu_ref, gu_in), (dm_ref, dm_in), (dmo_ref, dmo_in),
                (gm_ref, gm_in), (gmo_ref, gmo_in),
            )
        )
    ]
    for load in loads:
        load.start()

    def signal(sem, rep_, fsdp_):
        pl.semaphore_signal(
            sem, inc=1, device_id={"rep": rep_, "fsdp": fsdp_}, device_id_type=pl.DeviceIdType.MESH
        )

    near = [
        (rep, fs(zh, (x + 1) % 4, y)), (rep, fs(zh, (x + 3) % 4, y)),
        (rep, fs(zh, x, (y + 1) % 4)), (rep, fs(zh, x, (y + 3) % 4)),
    ]
    barrier = pltpu.get_barrier_semaphore()
    for peer in near + [(sibling, fsdp), on_line((z + 1) % 16), on_line((z + 15) % 16)]:
        signal(barrier, *peer)

    rounds = (
        near + [on_line((z + 1) % 16), on_line((z + 15) % 16)],
        [on_line((z + 2) % 16), on_line((z + 14) % 16)],
        [on_line((z + 4) % 16), on_line((z + 12) % 16)],
        [(sibling, fsdp)],
    )

    def tell(i):
        for peer in rounds[i]:
            signal(line.at[i], *peer)

    def hear(i):
        pl.semaphore_wait(line.at[i], len(rounds[i]))

    lane = lax.broadcasted_iota(jnp.int32, (8, 512), 1)
    lane8 = lax.broadcasted_iota(jnp.int32, (8, LANES), 1)

    def arrange(g):
        for h in range(2):
            zh_ = SHARD[g][h]
            for x_ in range(NX):
                for y_ in range(NY):
                    d1, d2 = (x_, y_) if h == 0 else (y_, x_)
                    col = ((zh_ * NX + x_) * NY + y_) * LANES
                    for c in range(2):
                        S[g, h, d1, d2, c, 0:32, :] = dn_in[0, 0, 32 * c : 32 * c + 32, col : col + LANES]
                for yp in range(NY // 2):
                    col = ((zh_ * NX + x_) * NY + 2 * yp) * GUCOLS
                    both = jnp.concatenate(
                        [gu_in[0, 0, i, :, col : col + 2 * GUCOLS].astype(F32) for i in range(2)], axis=0
                    )
                    odd = pltpu.roll(both[:, 384:896], 512 - HALF, 1)
                    for o, part in enumerate((both[:, 0:512], odd)):
                        part = jnp.where(lane < GUCOLS, part, 0.0)
                        y_ = 2 * yp + o
                        d1, d2 = (x_, y_) if h == 0 else (y_, x_)
                        for c in range(2):
                            two = jnp.concatenate(
                                [part[:, 256 * c : 256 * c + 128], part[:, 256 * c + 128 : 256 * c + 256]], axis=0
                            )
                            S[g, h, d1, d2, c, 32:48, :] = two.astype(BF)

    def ways(h):
        mine = along[h][0]
        return (
            (0, (mine + 1) % 4, pl.ds(0, 2), pl.ds(2, 2)),
            (1, (mine + 3) % 4, pl.ds(2, 2), pl.ds(0, 2)),
        )

    def ahead(g):
        for h in range(2):
            far = (along[h][0] + 2) % 4
            for w, near, on, _ in ways(h):
                remote(
                    S.at[g, h, far, on], RA.at[g, h, w], P1B + 2 * g + h, P1A + 4 * g + 2 * h + w,
                    rep, first_peer(h, near),
                ).start()

    def rest_of(g):
        for h in range(2):
            for w, near, _, rest in ways(h):
                sem = P1B + 2 * g + h
                remote(S.at[g, h, near, rest], R1.at[g, h, w, rest], sem, sem, rep, first_peer(h, near)).start()

    def pass_on(g):
        for h in range(2):
            for w, near, on, _ in ways(h):
                wait_bytes(RA.at[g, h, w], recv.at[P1A + 4 * g + 2 * h + w])
                S[g, h, near, on] = (S[g, h, near, on].astype(F32) + RA[g, h, w].astype(F32)).astype(BF)
                sem = P1B + 2 * g + h
                remote(S.at[g, h, near, on], R1.at[g, h, w, on], sem, sem, rep, first_peer(h, near)).start()

    def second_axis(g):
        for h in range(2):
            mine, other = along[h]
            sem = P2 + 2 * g + h
            wait_bytes(R1.at[g, h], recv.at[P1B + 2 * g + h])
            for d in (2, 1, 3, 0):
                dest = (other + d) % 4
                acc = S[g, h, mine, dest].astype(F32) + R1[g, h, 0, dest].astype(F32)
                acc = acc + R1[g, h, 1, dest].astype(F32)
                PS[g, h, dest] = acc.astype(BF)
                if d:
                    remote(PS.at[g, h, dest], R2.at[g, h, d - 1], sem, sem, rep, second_peer(h, dest)).start()

    def to_owners(g):
        for h in range(2):
            to = SHARD[g][h]
            wait_bytes(R2.at[g, h], recv.at[P2 + 2 * g + h])
            acc = PS[g, h, along[h][1]].astype(F32)
            for i in range(3):
                acc = acc + R2[g, h, i].astype(F32)
            Q[to] = acc.astype(BF)
            for c in range(2):
                copy = remote(Q.at[to, c], R3.at[2 * z + core], Z3, Z3, 2 * OWNER[c] + c, fs(to, x, y))
                pl.when(jnp.logical_or(fsdp != fs(to, x, y), rep != 2 * OWNER[c] + c))(copy.start)

    loads[0].wait()
    loads[1].wait()
    arrange(0)
    pl.semaphore_wait(barrier, 7)
    ahead(0)
    arrange(1)
    ahead(1)
    tell(0)
    rest_of(0)
    rest_of(1)
    hear(0)
    tell(1)
    pass_on(0)
    pass_on(1)
    for load in loads[2:]:
        load.wait()
    for g_ref, d_ref, out in ((gm_in, dm_in, M), (gmo_in, dmo_in, MO)):
        for c in range(2):
            for k in range(2):
                row = 32 * c + 16 * k
                out[c, 16 * k : 16 * k + 16, :] = d_ref[row : row + 16, :]
        for j in range(2):
            for t in range(4):
                row = 8 * (t % 2) + 4 * j
                if t < 3:
                    out[t // 2, 32 + row : 36 + row, :] = g_ref[j, :, 128 * t : 128 * t + 128]
                else:
                    out[1, 32 + row : 36 + row, :] = jnp.concatenate(
                        [g_ref[j, :, 384:448], jnp.zeros((4, HALF), F32)], axis=1
                    )
    hear(1)
    tell(2)
    second_axis(0)
    second_axis(1)
    hear(2)
    tell(3)
    hear(3)
    to_owners(0)
    to_owners(1)

    hh, gg = zh // 2, zh % 2
    d1 = jnp.where(hh == 0, x, y)

    @pl.when(owner)
    def _():
        R3[2 * z + core] = Q[zh, core]
        wait_bytes(R3.at[pl.ds(0, 31)], recv.at[Z3])
        largest = jnp.zeros((48, LANES), F32)
        total = jnp.zeros((48, LANES), F32)
        for r in range(8):
            part = R3[r].astype(F32)
            for k in range(1, 4):
                part = part + R3[8 * k + r].astype(F32)
            largest = jnp.maximum(largest, jnp.abs(part))
            total = total + part
        delta = total / 8
        moment = 0.9 * MO[core] + delta
        master = M[core] - 0.7 * (delta + 0.9 * moment)
        mine = G.at[core, gg, hh, d1, 0]
        mine[...] = master.astype(BF)
        for k in (8, 7, 9, 6, 10, 5, 11, 4, 12, 3, 13, 2, 14, 1, 15):
            remote(mine, mine, Z0, Z0 + gg, *on_line((z + k) % 16)).start()
        low = lax.broadcasted_iota(jnp.int32, (48, LANES), 1) < HALF
        low_max = jnp.max(jnp.where(low, largest, 0.0), axis=1, keepdims=True)
        high_max = jnp.max(jnp.where(low, 0.0, largest), axis=1, keepdims=True)
        D[core, 0] = delta
        D[core, 1] = jnp.where(low, low_max, high_max) + 1e-6

    def gather_second(g):
        made = jnp.logical_and(owner, gg == g)

        @pl.when(made)
        def _():
            wait_bytes(R3.at[0], recv.at[Z0 + g])

        @pl.when(jnp.logical_not(made))
        def _():
            wait_bytes(R3.at[pl.ds(0, 2)], recv.at[Z0 + g])

        for h in range(2):
            mine, other = along[h]
            sem = A1 + 2 * g + h
            block = G.at[core, g, h, mine, 0]
            for d in (2, 1, 3):
                to = second_peer(h, (other + d) % 4)
                remote(block, G.at[core, g, h, mine, 4 - d], sem, sem, rep, to).start()
        for h in range(2):
            mine = along[h][0]
            block = G.at[core, g, h, mine, 0]
            for d in (2, 1, 3):
                to = first_peer(h, (mine + d) % 4)
                remote(block, block, A1 + 2 * g + h, A2 + 6 * g + 3 * h + d - 1, rep, to).start()

    def to_sibling(g, h, d):
        block = G.at[core, g, h, d]
        remote(block, block, SC + 2 * g + h, SC + 2 * g + h, sibling, fsdp).start()

    def gather_first(g):
        for h in range(2):
            mine, other = along[h]
            wait_bytes(G.at[core, g, h, mine, pl.ds(1, 3)], recv.at[A1 + 2 * g + h])
            for d in (2, 1, 3):
                block = G.at[core, g, h, mine, pl.ds(1, 3)]
                remote(
                    block, block, A2 + 6 * g + 3 * h, A2 + 6 * g + 3 * h + d - 1,
                    rep, first_peer(h, (mine + d) % 4),
                ).start()
            to_sibling(g, h, mine)

    def share(g):
        for d in (1, 3, 2):
            for h in range(2):
                source = (along[h][0] + 4 - d) % 4
                wait_bytes(G.at[core, g, h, source], recv.at[A2 + 6 * g + 3 * h + d - 1])
                to_sibling(g, h, source)

    gather_second(0)
    gather_second(1)

    @pl.when(owner)
    def _():
        for k in range(1, 4):
            block = D.at[core]
            remote(block, block, SD, SD, ((zl + k) % ZL) * 2 + core, fsdp).start()

    gather_first(0)

    gather_first(1)
    share(0)

    @pl.when(jnp.logical_not(owner))
    def _():
        wait_bytes(D.at[core], recv.at[SD])

    remote(D.at[core], D.at[core], SDS, SDS, sibling, fsdp).start()

    def write(g, h):
        zh_ = SHARD[g][h]
        wait_bytes(G.at[1 - core, g, h], recv.at[SC + 2 * g + h])
        for x_ in range(NX):
            gu_tiles = []
            for y_ in range(NY):
                e1, e2 = (x_, (y_ + 4 - y) % 4) if h == 0 else (y_, (x_ + 4 - x) % 4)
                col = ((zh_ * NX + x_) * NY + y_) * LANES
                wide = []
                for c in range(2):
                    for k in range(2):
                        row = 32 * c + 16 * k
                        dn_out[row : row + 16, col : col + LANES] = G[c, g, h, e1, e2, 16 * k : 16 * k + 16]
                    tile = G[c, g, h, e1, e2, 32:48].astype(F32)
                    wide += [tile[0:8], tile[8:16]]
                gu_tiles.append(wide)
            for yp in range(NY // 2):
                even, odd = gu_tiles[2 * yp], gu_tiles[2 * yp + 1]
                odd = pltpu.roll(jnp.concatenate(odd, axis=1), HALF, 1)
                joined = jnp.where(lane8 < HALF, even[3], odd[:, 0:128])
                full = jnp.concatenate(even[:3] + [joined, odd[:, 128:512]], axis=1)
                col = ((zh_ * NX + x_) * NY + 2 * yp) * GUCOLS
                for j in range(2):
                    gu_out[j, :, col : col + 2 * GUCOLS] = full[4 * j : 4 * j + 4].astype(BF)

    write(0, 0)
    write(0, 1)
    share(1)

    wait_bytes(D.at[1 - core], recv.at[SDS])
    moments, masters, scales = [], [], []
    for c in range(2):
        delta, scale = D[c, 0], D[c, 1]
        moment = 0.9 * MO[c] + delta
        master = M[c] - 0.7 * (delta + 0.9 * moment)
        for tiles, value in ((moments, moment), (masters, master), (scales, scale)):
            tiles.append([value[16 * k : 16 * k + 16] for k in range(OWN)])
    for tiles, d_out, g_out in ((moments, dmo_out, gmo_out), (masters, dm_out, gm_out)):
        for c in range(2):
            for k in range(2):
                row = 32 * c + 16 * k
                d_out[row : row + 16, :] = tiles[c][k]
        for j in range(2):
            for t in range(4):
                row = 8 * (t % 2) + 4 * j
                width = 128 if t < 3 else 64
                g_out[j, :, 128 * t : 128 * t + width] = tiles[t // 2][2][row : row + 4, :width]
    rows = jnp.concatenate([scales[c][k] for c in range(2) for k in range(2)], axis=0)
    lane64 = lax.broadcasted_iota(jnp.int32, (64, LANES), 1)
    pair = jnp.where(lane64 == 0, rows, pltpu.roll(rows, HALF, 1))
    ds_out[...] = pair.T[0:2, :]
    acc = jnp.zeros((8, LANES), F32)
    for t in range(4):
        tile = scales[t // 2][2][8 * (t % 2) : 8 * (t % 2) + 8]
        acc = jnp.where(lane8 == 2 * t, tile, acc)
        acc = jnp.where(lane8 == 2 * t + 1, pltpu.roll(tile, HALF, 1), acc)
    for j in range(2):
        gs_out[j, :, :] = acc[4 * j : 4 * j + 4, 0:7]

    write(1, 0)
    write(1, 1)

    for g, h in pairs:
        i = 2 * g + h
        wait_bytes(S.at[g, h, pl.ds(0, 3)], send.at[P1B + i])
        wait_bytes(R2.at[g, h], send.at[P2 + i])
        wait_bytes(R3.at[pl.ds(0, 6)], send.at[A1 + i])
        wait_bytes(R3.at[pl.ds(0, 9)], send.at[A2 + 3 * i])
        wait_bytes(G.at[core, g, h], send.at[SC + i])
    wait_bytes(D.at[core], send.at[SDS])

    @pl.when(owner)
    def _():
        wait_bytes(R3.at[pl.ds(0, 7)], send.at[Z3])
        wait_bytes(R3.at[pl.ds(0, 15)], send.at[Z0])
        wait_bytes(R3.at[pl.ds(0, 12)], send.at[SD])

    @pl.when(jnp.logical_not(owner))
    def _():
        wait_bytes(R3.at[pl.ds(0, 8)], send.at[Z3])


def place(*refs):
    n = (len(refs) - 1) // 2
    copies = [pltpu.make_async_copy(refs[i], refs[n + i], refs[-1].at[i]) for i in range(n)]
    for copy in copies:
        copy.start()
    for copy in copies:
        copy.wait()


def per_device(gu_pseudo, gu_master, gu_moment, down_pseudo, down_master, down_moment):
    shapes = (
        jax.ShapeDtypeStruct(gu_pseudo.shape[2:], BF),
        jax.ShapeDtypeStruct(down_pseudo.shape[2:], BF),
        jax.ShapeDtypeStruct(gu_master.shape, F32),
        jax.ShapeDtypeStruct(down_master.shape, F32),
        jax.ShapeDtypeStruct(gu_master.shape, F32),
        jax.ShapeDtypeStruct(down_master.shape, F32),
        jax.ShapeDtypeStruct(gu_master.shape[:2] + (7,), F32),
        jax.ShapeDtypeStruct((2, down_master.shape[0]), F32),
    )
    operands = [
        pltpu.with_memory_space_constraint(a, pltpu.HBM)
        for a in (gu_pseudo, gu_master, gu_moment, down_pseudo, down_master, down_moment)
    ]
    vmem = pl.BlockSpec(memory_space=pltpu.VMEM)
    hbm = pl.BlockSpec(memory_space=pl.ANY)
    results = pl.pallas_call(
        kernel,
        out_shape=shapes,
        in_specs=[hbm] * 6,
        out_specs=[vmem] * 8,
        scratch_shapes=[
            pltpu.VMEM(gu_pseudo.shape, BF),
            pltpu.VMEM(down_pseudo.shape, BF),
            pltpu.VMEM(gu_master.shape, F32),
            pltpu.VMEM(gu_master.shape, F32),
            pltpu.VMEM(down_master.shape, F32),
            pltpu.VMEM(down_master.shape, F32),
            pltpu.VMEM((2, 2, 4, 4, 2, 48, LANES), BF),
            pltpu.VMEM((2, 2, 2, 2, 2, 48, LANES), BF),
            pltpu.VMEM((2, 2, 2, 4, 2, 48, LANES), BF),
            pltpu.VMEM((2, 2, 4, 2, 48, LANES), BF),
            pltpu.VMEM((2, 2, 3, 2, 48, LANES), BF),
            pltpu.VMEM((4, 2, 48, LANES), BF),
            pltpu.VMEM((32, 48, LANES), BF),
            pltpu.VMEM((2, 2, 48, LANES), F32),
            pltpu.VMEM((2, 2, 2, 4, 4, 48, LANES), BF),
            pltpu.VMEM((2, 48, LANES), F32),
            pltpu.VMEM((2, 48, LANES), F32),
            pltpu.SemaphoreType.DMA((NSEM,)),
            pltpu.SemaphoreType.DMA((NSEM,)),
            pltpu.SemaphoreType.DMA((6,)),
            pltpu.SemaphoreType.REGULAR((4,)),
        ],
        compiler_params=pltpu.CompilerParams(
            collective_id=0, has_side_effects=True, vmem_limit_bytes=40 * MIB
        ),
    )(*operands)
    results = pl.pallas_call(
        place,
        out_shape=shapes,
        in_specs=[vmem] * 8,
        out_specs=[hbm] * 8,
        scratch_shapes=[pltpu.SemaphoreType.DMA((8,))],
        compiler_params=pltpu.CompilerParams(vmem_limit_bytes=40 * MIB),
    )(*results)
    return tuple(results[:7]) + (results[7].T,)


def solution(mesh):
    in_specs = (
        P("rep", "fsdp", None, None, None),
        P(None, None, "fsdp"),
        P(None, None, "fsdp"),
        P("rep", "fsdp", None, None),
        P(None, "fsdp"),
        P(None, "fsdp"),
    )
    out_specs = (
        P(),
        P(),
        P(None, None, "fsdp"),
        P(None, "fsdp"),
        P(None, None, "fsdp"),
        P(None, "fsdp"),
        P(None, None, "fsdp"),
        P(None, "fsdp"),
    )
    return jax.shard_map(
        per_device, mesh=mesh, in_specs=in_specs, out_specs=out_specs, check_vma=False
    )
```

```python
import jax
import jax.numpy as jnp
from jax import lax
from jax.experimental import pallas as pl
from jax.experimental.pallas import tpu as pltpu
from jax.sharding import PartitionSpec as P

NX = 4
NY = 4
ZH = 4
ZL = 4
LANES = 128
HALF = 64
GUCOLS = 448
OWN = 3
SHARD = ((0, 2), (1, 3))
OWNER = (2, 0)
BF = jnp.bfloat16
F32 = jnp.float32
MIB = 1024 * 1024

P1A, P1B, P2, Z3, Z0, SD, SDS, A1, A2, SC = 0, 8, 12, 16, 17, 19, 20, 21, 25, 37
NSEM = 41


def kernel(
    gu_ref, gm_ref, gmo_ref, dn_ref, dm_ref, dmo_ref,
    gu_out, dn_out, gm_out, dm_out, gmo_out, dmo_out, gs_out, ds_out,
    gu_in, dn_in, gm_in, gmo_in, dm_in, dmo_in,
    S, RA, R1, PS, R2, Q, R3, D, G, M, MO, send, recv, local, line,
):
    rep = lax.axis_index("rep")
    fsdp = lax.axis_index("fsdp")
    zl, core = rep // 2, rep % 2
    zh, x, y = fsdp // (NX * NY), (fsdp // NY) % NX, fsdp % NY
    z = zh * ZL + zl
    along = ((x, y), (y, x))
    sibling = zl * 2 + (1 - core)
    owner = zl == OWNER[0] + core * (OWNER[1] - OWNER[0])
    pairs = [(g, h) for g in range(2) for h in range(2)]

    def fs(zh_, x_, y_):
        return (zh_ * NX + x_) * NY + y_

    def first_peer(h, d):
        return fs(zh, d, y) if h == 0 else fs(zh, x, d)

    def second_peer(h, d):
        return fs(zh, x, d) if h == 0 else fs(zh, d, y)

    def on_line(oz):
        return (oz % ZL) * 2 + core, fs(oz // ZL, x, y)

    def remote(src, dst, out, sem, rep_, fsdp_):
        return pltpu.make_async_remote_copy(
            src_ref=src, dst_ref=dst, send_sem=send.at[out], recv_sem=recv.at[sem],
            device_id={"rep": rep_, "fsdp": fsdp_}, device_id_type=pl.DeviceIdType.MESH,
        )

    def wait_bytes(ref, sem):
        pltpu.make_async_copy(ref, ref, sem).wait()

    loads = [
        pltpu.make_async_copy(src, dst, local.at[i])
        for i, (src, dst) in enumerate(
            (
                (dn_ref, dn_in), (gu_ref, gu_in), (dm_ref, dm_in), (dmo_ref, dmo_in),
                (gm_ref, gm_in), (gmo_ref, gmo_in),
            )
        )
    ]
    for load in loads:
        load.start()

    def signal(sem, rep_, fsdp_):
        pl.semaphore_signal(
            sem, inc=1, device_id={"rep": rep_, "fsdp": fsdp_}, device_id_type=pl.DeviceIdType.MESH
        )

    near = [
        (rep, fs(zh, (x + 1) % 4, y)), (rep, fs(zh, (x + 3) % 4, y)),
        (rep, fs(zh, x, (y + 1) % 4)), (rep, fs(zh, x, (y + 3) % 4)),
    ]
    barrier = pltpu.get_barrier_semaphore()
    for peer in near + [(sibling, fsdp), on_line((z + 1) % 16), on_line((z + 15) % 16)]:
        signal(barrier, *peer)

    rounds = (
        near + [on_line((z + 1) % 16), on_line((z + 15) % 16)],
        [on_line((z + 2) % 16), on_line((z + 14) % 16)],
        [on_line((z + 4) % 16), on_line((z + 12) % 16)],
        [(sibling, fsdp)],
    )

    def tell(i):
        for peer in rounds[i]:
            signal(line.at[i], *peer)

    def hear(i):
        pl.semaphore_wait(line.at[i], len(rounds[i]))

    lane = lax.broadcasted_iota(jnp.int32, (8, 512), 1)
    lane8 = lax.broadcasted_iota(jnp.int32, (8, LANES), 1)

    def arrange(g):
        for h in range(2):
            zh_ = SHARD[g][h]
            for x_ in range(NX):
                for y_ in range(NY):
                    d1, d2 = (x_, y_) if h == 0 else (y_, x_)
                    col = ((zh_ * NX + x_) * NY + y_) * LANES
                    for c in range(2):
                        S[g, h, d1, d2, c, 0:32, :] = dn_in[0, 0, 32 * c : 32 * c + 32, col : col + LANES]
                for yp in range(NY // 2):
                    col = ((zh_ * NX + x_) * NY + 2 * yp) * GUCOLS
                    both = jnp.concatenate(
                        [gu_in[0, 0, i, :, col : col + 2 * GUCOLS].astype(F32) for i in range(2)], axis=0
                    )
                    odd = pltpu.roll(both[:, 384:896], 512 - HALF, 1)
                    for o, part in enumerate((both[:, 0:512], odd)):
                        part = jnp.where(lane < GUCOLS, part, 0.0)
                        y_ = 2 * yp + o
                        d1, d2 = (x_, y_) if h == 0 else (y_, x_)
                        for c in range(2):
                            two = jnp.concatenate(
                                [part[:, 256 * c : 256 * c + 128], part[:, 256 * c + 128 : 256 * c + 256]], axis=0
                            )
                            S[g, h, d1, d2, c, 32:48, :] = two.astype(BF)

    def ways(h):
        mine = along[h][0]
        return (
            (0, (mine + 1) % 4, pl.ds(0, 2), pl.ds(2, 2)),
            (1, (mine + 3) % 4, pl.ds(2, 2), pl.ds(0, 2)),
        )

    def ahead(g):
        for h in range(2):
            far = (along[h][0] + 2) % 4
            for w, near, on, _ in ways(h):
                remote(
                    S.at[g, h, far, on], RA.at[g, h, w], P1B + 2 * g + h, P1A + 4 * g + 2 * h + w,
                    rep, first_peer(h, near),
                ).start()

    def rest_of(g):
        for h in range(2):
            for w, near, _, rest in ways(h):
                sem = P1B + 2 * g + h
                remote(S.at[g, h, near, rest], R1.at[g, h, w, rest], sem, sem, rep, first_peer(h, near)).start()

    def pass_on(g):
        for h in range(2):
            for w, near, on, _ in ways(h):
                wait_bytes(RA.at[g, h, w], recv.at[P1A + 4 * g + 2 * h + w])
                S[g, h, near, on] = (S[g, h, near, on].astype(F32) + RA[g, h, w].astype(F32)).astype(BF)
                sem = P1B + 2 * g + h
                remote(S.at[g, h, near, on], R1.at[g, h, w, on], sem, sem, rep, first_peer(h, near)).start()

    def second_axis(g):
        for h in range(2):
            mine, other = along[h]
            sem = P2 + 2 * g + h
            wait_bytes(R1.at[g, h], recv.at[P1B + 2 * g + h])
            for d in (2, 1, 3, 0):
                dest = (other + d) % 4
                acc = S[g, h, mine, dest].astype(F32) + R1[g, h, 0, dest].astype(F32)
                acc = acc + R1[g, h, 1, dest].astype(F32)
                PS[g, h, dest] = acc.astype(BF)
                if d:
                    remote(PS.at[g, h, dest], R2.at[g, h, d - 1], sem, sem, rep, second_peer(h, dest)).start()

    def to_owners(g):
        for h in range(2):
            to = SHARD[g][h]
            wait_bytes(R2.at[g, h], recv.at[P2 + 2 * g + h])
            acc = PS[g, h, along[h][1]].astype(F32)
            for i in range(3):
                acc = acc + R2[g, h, i].astype(F32)
            Q[to] = acc.astype(BF)
            for c in range(2):
                copy = remote(Q.at[to, c], R3.at[2 * z + core], Z3, Z3, 2 * OWNER[c] + c, fs(to, x, y))
                pl.when(jnp.logical_or(fsdp != fs(to, x, y), rep != 2 * OWNER[c] + c))(copy.start)

    loads[0].wait()
    loads[1].wait()
    arrange(0)
    pl.semaphore_wait(barrier, 7)
    ahead(0)
    arrange(1)
    ahead(1)
    tell(0)
    rest_of(0)
    rest_of(1)
    hear(0)
    tell(1)
    pass_on(0)
    pass_on(1)
    for load in loads[2:]:
        load.wait()
    for g_ref, d_ref, out in ((gm_in, dm_in, M), (gmo_in, dmo_in, MO)):
        for c in range(2):
            for k in range(2):
                row = 32 * c + 16 * k
                out[c, 16 * k : 16 * k + 16, :] = d_ref[row : row + 16, :]
        for j in range(2):
            for t in range(4):
                row = 8 * (t % 2) + 4 * j
                if t < 3:
                    out[t // 2, 32 + row : 36 + row, :] = g_ref[j, :, 128 * t : 128 * t + 128]
                else:
                    out[1, 32 + row : 36 + row, :] = jnp.concatenate(
                        [g_ref[j, :, 384:448], jnp.zeros((4, HALF), F32)], axis=1
                    )
    hear(1)
    tell(2)
    second_axis(0)
    second_axis(1)
    hear(2)
    tell(3)
    hear(3)
    to_owners(0)
    to_owners(1)

    hh, gg = zh // 2, zh % 2
    d1 = jnp.where(hh == 0, x, y)

    @pl.when(owner)
    def _():
        R3[2 * z + core] = Q[zh, core]
        wait_bytes(R3.at[pl.ds(0, 31)], recv.at[Z3])
        largest = jnp.zeros((48, LANES), F32)
        total = jnp.zeros((48, LANES), F32)
        for r in range(8):
            part = R3[r].astype(F32)
            for k in range(1, 4):
                part = part + R3[8 * k + r].astype(F32)
            largest = jnp.maximum(largest, jnp.abs(part))
            total = total + part
        delta = total / 8
        moment = 0.9 * MO[core] + delta
        master = M[core] - 0.7 * (delta + 0.9 * moment)
        mine = G.at[core, gg, hh, d1, 0]
        mine[...] = master.astype(BF)
        for k in (8, 7, 9, 6, 10, 5, 11, 4, 12, 3, 13, 2, 14, 1, 15):
            remote(mine, mine, Z0, Z0 + gg, *on_line((z + k) % 16)).start()
        low = lax.broadcasted_iota(jnp.int32, (48, LANES), 1) < HALF
        low_max = jnp.max(jnp.where(low, largest, 0.0), axis=1, keepdims=True)
        high_max = jnp.max(jnp.where(low, 0.0, largest), axis=1, keepdims=True)
        D[core, 0] = delta
        D[core, 1] = jnp.where(low, low_max, high_max) + 1e-6

    def gather_second(g):
        made = jnp.logical_and(owner, gg == g)

        @pl.when(made)
        def _():
            wait_bytes(R3.at[0], recv.at[Z0 + g])

        @pl.when(jnp.logical_not(made))
        def _():
            wait_bytes(R3.at[pl.ds(0, 2)], recv.at[Z0 + g])

        for h in range(2):
            mine, other = along[h]
            sem = A1 + 2 * g + h
            block = G.at[core, g, h, mine, 0]
            for d in (2, 1, 3):
                to = second_peer(h, (other + d) % 4)
                remote(block, G.at[core, g, h, mine, 4 - d], sem, sem, rep, to).start()
        for h in range(2):
            mine = along[h][0]
            block = G.at[core, g, h, mine, 0]
            for d in (2, 1, 3):
                to = first_peer(h, (mine + d) % 4)
                remote(block, block, A1 + 2 * g + h, A2 + 6 * g + 3 * h + d - 1, rep, to).start()

    def to_sibling(g, h, d):
        block = G.at[core, g, h, d]
        remote(block, block, SC + 2 * g + h, SC + 2 * g + h, sibling, fsdp).start()

    def gather_first(g):
        for h in range(2):
            mine, other = along[h]
            wait_bytes(G.at[core, g, h, mine, pl.ds(1, 3)], recv.at[A1 + 2 * g + h])
            for d in (2, 1, 3):
                block = G.at[core, g, h, mine, pl.ds(1, 3)]
                remote(
                    block, block, A2 + 6 * g + 3 * h, A2 + 6 * g + 3 * h + d - 1,
                    rep, first_peer(h, (mine + d) % 4),
                ).start()
            to_sibling(g, h, mine)

    def share(g):
        for d in (1, 3, 2):
            for h in range(2):
                source = (along[h][0] + 4 - d) % 4
                wait_bytes(G.at[core, g, h, source], recv.at[A2 + 6 * g + 3 * h + d - 1])
                to_sibling(g, h, source)

    gather_second(0)
    gather_second(1)

    @pl.when(owner)
    def _():
        for k in range(1, 4):
            block = D.at[core]
            remote(block, block, SD, SD, ((zl + k) % ZL) * 2 + core, fsdp).start()

    gather_first(0)

    gather_first(1)
    share(0)

    @pl.when(jnp.logical_not(owner))
    def _():
        wait_bytes(D.at[core], recv.at[SD])

    remote(D.at[core], D.at[core], SDS, SDS, sibling, fsdp).start()

    def write(g, h):
        zh_ = SHARD[g][h]
        wait_bytes(G.at[1 - core, g, h], recv.at[SC + 2 * g + h])
        for x_ in range(NX):
            gu_tiles = []
            for y_ in range(NY):
                e1, e2 = (x_, (y_ + 4 - y) % 4) if h == 0 else (y_, (x_ + 4 - x) % 4)
                col = ((zh_ * NX + x_) * NY + y_) * LANES
                wide = []
                for c in range(2):
                    for k in range(2):
                        row = 32 * c + 16 * k
                        dn_out[row : row + 16, col : col + LANES] = G[c, g, h, e1, e2, 16 * k : 16 * k + 16]
                    tile = G[c, g, h, e1, e2, 32:48].astype(F32)
                    wide += [tile[0:8], tile[8:16]]
                gu_tiles.append(wide)
            for yp in range(NY // 2):
                even, odd = gu_tiles[2 * yp], gu_tiles[2 * yp + 1]
                odd = pltpu.roll(jnp.concatenate(odd, axis=1), HALF, 1)
                joined = jnp.where(lane8 < HALF, even[3], odd[:, 0:128])
                full = jnp.concatenate(even[:3] + [joined, odd[:, 128:512]], axis=1)
                col = ((zh_ * NX + x_) * NY + 2 * yp) * GUCOLS
                for j in range(2):
                    gu_out[j, :, col : col + 2 * GUCOLS] = full[4 * j : 4 * j + 4].astype(BF)

    write(0, 0)
    write(0, 1)
    for g, h in pairs:
        i = 2 * g + h
        wait_bytes(S.at[g, h, pl.ds(0, 3)], send.at[P1B + i])
        wait_bytes(R2.at[g, h], send.at[P2 + i])
        wait_bytes(R3.at[pl.ds(0, 6)], send.at[A1 + i])

    @pl.when(owner)
    def _():
        wait_bytes(R3.at[pl.ds(0, 7)], send.at[Z3])
        wait_bytes(R3.at[pl.ds(0, 15)], send.at[Z0])
        wait_bytes(R3.at[pl.ds(0, 12)], send.at[SD])

    @pl.when(jnp.logical_not(owner))
    def _():
        wait_bytes(R3.at[pl.ds(0, 8)], send.at[Z3])

    share(1)

    wait_bytes(D.at[1 - core], recv.at[SDS])
    moments, masters, scales = [], [], []
    for c in range(2):
        delta, scale = D[c, 0], D[c, 1]
        moment = 0.9 * MO[c] + delta
        master = M[c] - 0.7 * (delta + 0.9 * moment)
        for tiles, value in ((moments, moment), (masters, master), (scales, scale)):
            tiles.append([value[16 * k : 16 * k + 16] for k in range(OWN)])
    for tiles, d_out, g_out in ((moments, dmo_out, gmo_out), (masters, dm_out, gm_out)):
        for c in range(2):
            for k in range(2):
                row = 32 * c + 16 * k
                d_out[row : row + 16, :] = tiles[c][k]
        for j in range(2):
            for t in range(4):
                row = 8 * (t % 2) + 4 * j
                width = 128 if t < 3 else 64
                g_out[j, :, 128 * t : 128 * t + width] = tiles[t // 2][2][row : row + 4, :width]
    rows = jnp.concatenate([scales[c][k] for c in range(2) for k in range(2)], axis=0)
    lane64 = lax.broadcasted_iota(jnp.int32, (64, LANES), 1)
    pair = jnp.where(lane64 == 0, rows, pltpu.roll(rows, HALF, 1))
    ds_out[...] = pair.T[0:2, :]
    acc = jnp.zeros((8, LANES), F32)
    for t in range(4):
        tile = scales[t // 2][2][8 * (t % 2) : 8 * (t % 2) + 8]
        acc = jnp.where(lane8 == 2 * t, tile, acc)
        acc = jnp.where(lane8 == 2 * t + 1, pltpu.roll(tile, HALF, 1), acc)
    for j in range(2):
        gs_out[j, :, :] = acc[4 * j : 4 * j + 4, 0:7]

    write(1, 0)
    write(1, 1)

    for g, h in pairs:
        i = 2 * g + h
        wait_bytes(R3.at[pl.ds(0, 9)], send.at[A2 + 3 * i])
        wait_bytes(G.at[core, g, h], send.at[SC + i])
    wait_bytes(D.at[core], send.at[SDS])


def place(*refs):
    n = (len(refs) - 1) // 2
    copies = [pltpu.make_async_copy(refs[i], refs[n + i], refs[-1].at[i]) for i in range(n)]
    for copy in copies:
        copy.start()
    for copy in copies:
        copy.wait()


def per_device(gu_pseudo, gu_master, gu_moment, down_pseudo, down_master, down_moment):
    shapes = (
        jax.ShapeDtypeStruct(gu_pseudo.shape[2:], BF),
        jax.ShapeDtypeStruct(down_pseudo.shape[2:], BF),
        jax.ShapeDtypeStruct(gu_master.shape, F32),
        jax.ShapeDtypeStruct(down_master.shape, F32),
        jax.ShapeDtypeStruct(gu_master.shape, F32),
        jax.ShapeDtypeStruct(down_master.shape, F32),
        jax.ShapeDtypeStruct(gu_master.shape[:2] + (7,), F32),
        jax.ShapeDtypeStruct((2, down_master.shape[0]), F32),
    )
    operands = [
        pltpu.with_memory_space_constraint(a, pltpu.HBM)
        for a in (gu_pseudo, gu_master, gu_moment, down_pseudo, down_master, down_moment)
    ]
    vmem = pl.BlockSpec(memory_space=pltpu.VMEM)
    hbm = pl.BlockSpec(memory_space=pl.ANY)
    results = pl.pallas_call(
        kernel,
        out_shape=shapes,
        in_specs=[hbm] * 6,
        out_specs=[vmem] * 8,
        scratch_shapes=[
            pltpu.VMEM(gu_pseudo.shape, BF),
            pltpu.VMEM(down_pseudo.shape, BF),
            pltpu.VMEM(gu_master.shape, F32),
            pltpu.VMEM(gu_master.shape, F32),
            pltpu.VMEM(down_master.shape, F32),
            pltpu.VMEM(down_master.shape, F32),
            pltpu.VMEM((2, 2, 4, 4, 2, 48, LANES), BF),
            pltpu.VMEM((2, 2, 2, 2, 2, 48, LANES), BF),
            pltpu.VMEM((2, 2, 2, 4, 2, 48, LANES), BF),
            pltpu.VMEM((2, 2, 4, 2, 48, LANES), BF),
            pltpu.VMEM((2, 2, 3, 2, 48, LANES), BF),
            pltpu.VMEM((4, 2, 48, LANES), BF),
            pltpu.VMEM((32, 48, LANES), BF),
            pltpu.VMEM((2, 2, 48, LANES), F32),
            pltpu.VMEM((2, 2, 2, 4, 4, 48, LANES), BF),
            pltpu.VMEM((2, 48, LANES), F32),
            pltpu.VMEM((2, 48, LANES), F32),
            pltpu.SemaphoreType.DMA((NSEM,)),
            pltpu.SemaphoreType.DMA((NSEM,)),
            pltpu.SemaphoreType.DMA((6,)),
            pltpu.SemaphoreType.REGULAR((4,)),
        ],
        compiler_params=pltpu.CompilerParams(
            collective_id=0, has_side_effects=True, vmem_limit_bytes=40 * MIB
        ),
    )(*operands)
    results = pl.pallas_call(
        place,
        out_shape=shapes,
        in_specs=[vmem] * 8,
        out_specs=[hbm] * 8,
        scratch_shapes=[pltpu.SemaphoreType.DMA((8,))],
        compiler_params=pltpu.CompilerParams(vmem_limit_bytes=40 * MIB),
    )(*results)
    return tuple(results[:7]) + (results[7].T,)


def solution(mesh):
    in_specs = (
        P("rep", "fsdp", None, None, None),
        P(None, None, "fsdp"),
        P(None, None, "fsdp"),
        P("rep", "fsdp", None, None),
        P(None, "fsdp"),
        P(None, "fsdp"),
    )
    out_specs = (
        P(),
        P(),
        P(None, None, "fsdp"),
        P(None, "fsdp"),
        P(None, None, "fsdp"),
        P(None, "fsdp"),
        P(None, None, "fsdp"),
        P(None, "fsdp"),
    )
    return jax.shard_map(
        per_device, mesh=mesh, in_specs=in_specs, out_specs=out_specs, check_vma=False
    )
```
